128 devices in a mesh: pipe: 4 (over z_hi, core), dp: 32 (over z_lo, y, x).
Axes of the slice: x: 4, y: 4, z: 4 (z_hi: 2, z_lo: 2; z = z_hi * 2 + z_lo), core: 2. Of those that a mesh axis runs over, the one named last changes fastest.
Arguments:
- batches: bfloat16 [2, 128, 8192], P(None, None, 'dp'), may hold values from -6 to 6
- cotangents: bfloat16 [2, 128, 8192], P(None, None, 'dp'), may hold values from -1.5 to 1.5
- weights: bfloat16 [2, 4, 8192, 8192], P(None, 'pipe', None, 'dp'), may hold values from -0.044194174 to 0.54419417
- gains: bfloat16 [2, 4, 8192], P(None, 'pipe', 'dp'), may hold values from 0.4 to 3
- exponents: int32 [4, 64, 64], P('pipe', None, 'dp'), may hold values from -1 to 2
Outputs:
- weight_grads: bfloat16 [4, 8192, 8192], P('pipe', None, 'dp')
- last_states: bfloat16 [4, 128, 8192], P('pipe', None, 'dp')
The draws below stay inside these ranges and needn't reach their ends.
All inputs are finite; a program needn't handle non-finite values.
Results may differ from the reference program's by a relative error of at most 0.025.
Values may be sent and summed in bfloat16 or wider, within the bound.
No kernel may reach another device: no remote copies, remote signals or barrier semaphores. Data moves between devices by JAX's collectives and lax.ppermute only.
A program may use at most 128 MiB of HBM per device.

```python
import jax
import jax.numpy as jnp
from jax import lax

D = 8192
MICRO = 128
TILE = 128
N_PIPE = 4
N_DP = 32


def shared_inputs(key):
    return jnp.clip(jax.random.normal(key, (2, MICRO, D), jnp.float32), -4.0, 4.0)


def draw_batches(key, part):
    base = shared_inputs(key)
    return base.astype(jnp.bfloat16)


def draw_cotangents(key, part):
    base = shared_inputs(key)
    key = jax.random.fold_in(key, 12)
    noise = jnp.clip(jax.random.normal(key, (2, MICRO, D), jnp.float32), -4.0, 4.0)
    mixed = 0.1 * noise + 0.15 * base
    return jnp.clip(mixed, -1.5, 1.5).astype(jnp.bfloat16)


def draw_weights(key, part):
    key = jax.random.fold_in(key, 13)
    noise = jnp.clip(jax.random.normal(key, (2, N_PIPE, D, D), jnp.float32), -4.0, 4.0) / jnp.sqrt(jnp.float32(D))
    rows_idx = lax_iota_rows()
    diag = jnp.where(rows_idx[:, None] == rows_idx[None, :], 0.5, 0.0).astype(jnp.float32)
    return (noise + diag[None, None]).astype(jnp.bfloat16)


def lax_iota_rows():
    return jnp.arange(D, dtype=jnp.int32)


def draw_gains(key, part):
    key = jax.random.fold_in(key, 14)
    position = jnp.arange(D, dtype=jnp.float32) / (D - 1)
    ramp = 0.6 * jnp.exp(position * jnp.log(3.0))
    jitter = 1.0 + 0.1 * jnp.clip(jax.random.normal(key, (2, N_PIPE, D), jnp.float32), -2.0, 2.0)
    return jnp.clip(ramp[None, None] * jitter, 0.4, 3.0).astype(jnp.bfloat16)


def plant(entries, own_key, smallest, high):
    shape = entries.shape
    index_at = [jax.random.randint(jax.random.fold_in(own_key, axis), (), 0, shape[axis]) for axis in range(len(shape))]
    entries = entries.at[tuple(index_at)].set(smallest)
    longest = shape.index(max(shape))
    index_at[longest] = (index_at[longest] + 1) % shape[longest]
    return entries.at[tuple(index_at)].set(high)


def setup_inputs(seed: int = 0) -> dict:
    key_list = jax.random.split(jax.random.key(seed), 6)
    return {
        "batches": draw_batches(jax.random.fold_in(key_list[5], 71), 0),
        "cotangents": draw_cotangents(jax.random.fold_in(key_list[5], 71), 0),
        "weights": draw_weights(jax.random.fold_in(key_list[5], 71), 0),
        "gains": draw_gains(jax.random.fold_in(key_list[5], 71), 0),
        "exponents": plant(jax.random.randint(key_list[4], (N_PIPE, D // TILE, D // TILE), -1, 3), jax.random.fold_in(key_list[4], 1), -1, 2).astype(jnp.int32),
    }


def section_forward(x, weight, gain):
    x32 = x.astype(jnp.float32)
    scale = lax.rsqrt(lax.optimization_barrier(jnp.sum(x32 * x32, axis=1)) / D + 1e-05)
    normed = x32 * scale[:, None]
    features = (normed * gain.astype(jnp.float32)).astype(jnp.bfloat16)
    out = (x32 + jnp.dot(features, weight, preferred_element_type=jnp.float32)).astype(jnp.bfloat16)
    return (out, (normed, scale, features))

def section_backward(g_out, weight, gain, saved):
    normed, scale, features = saved
    grad_w = jnp.dot(features.T, g_out, preferred_element_type=jnp.float32)
    width = D // N_DP
    blocks_g = g_out.astype(jnp.float32).reshape(MICRO, N_DP, width)
    blocks_w = weight.astype(jnp.float32).reshape(D, N_DP, width)
    partial_value = jnp.einsum('mjk,djk->jmd', blocks_g, blocks_w)
    partial_value = lax.optimization_barrier(partial_value.astype(jnp.bfloat16))
    grad_feat = lax.optimization_barrier(jnp.sum(partial_value.astype(jnp.float32), axis=0))
    grad_norm = grad_feat * gain.astype(jnp.float32)
    mix = lax.optimization_barrier(jnp.sum(grad_norm * normed, axis=1)) / D
    grad_in = (g_out.astype(jnp.float32) + scale[:, None] * (grad_norm - normed * mix[:, None])).astype(jnp.bfloat16)
    return (grad_in, grad_w)

def run_batch(start, cotangent, weight_list, gain_list):
    state = start
    saved_list = []
    outputs = []
    for section in range(N_PIPE):
        state, saved = section_forward(state, weight_list[section], gain_list[section])
        saved_list.append(saved)
        outputs.append(state)
    grads = [None] * N_PIPE
    g_out = cotangent
    for section in reversed(range(N_PIPE)):
        g_out, grads[section] = section_backward(g_out, weight_list[section], gain_list[section], saved_list[section])
    return (outputs, grads)

def reference(batches, cotangents, weights, gains, exponents):
    down_weights = [weights[0, section] for section in range(N_PIPE)]
    down_gains = [gains[0, section] for section in range(N_PIPE)]
    up_weights = [weights[1, N_PIPE - 1 - section] for section in range(N_PIPE)]
    up_gains = [gains[1, N_PIPE - 1 - section] for section in range(N_PIPE)]
    outs_down, grads_down = run_batch(batches[0], cotangents[0], down_weights, down_gains)
    outs_up, grads_up = run_batch(batches[1], cotangents[1], up_weights, up_gains)
    rows = []
    grad_rows = []
    for section in range(N_PIPE):
        if section >= N_PIPE // 2:
            rows.append(outs_down[section])
        else:
            rows.append(outs_up[N_PIPE - 1 - section])
        returned = lax.optimization_barrier(grads_up[section].astype(jnp.bfloat16)).astype(jnp.float32)
        expanded = jnp.repeat(jnp.repeat(exponents[section], TILE, axis=0), TILE, axis=1)
        factor = jnp.exp2(-expanded.astype(jnp.float32))
        grad_rows.append(((grads_down[section] + returned) * factor).astype(jnp.bfloat16))
    return (jnp.stack(grad_rows), jnp.stack(rows))
```

```python
import functools

import jax
import jax.numpy as jnp
from jax import lax
from jax.experimental import pallas as pl
from jax.experimental.pallas import tpu as pltpu
from jax.sharding import PartitionSpec as P

D = 8192
EPS = 1e-05
M = 128
H = 128
N = 32
R = M + 16
F32 = jnp.float32
BF16 = jnp.bfloat16
BOTH = ("pipe", "dp")
VM = pl.BlockSpec(memory_space=pltpu.VMEM)
HBM = pl.BlockSpec(memory_space=pl.ANY)
PARAMS = pltpu.CompilerParams(vmem_limit_bytes=56 * 1024 * 1024)


def pairs(fn):
    out = []
    for i in range(128):
        p, d = divmod(i, 32)
        zh, c = divmod(p, 2)
        zl, r = divmod(d, 16)
        y, x = divmod(r, 4)
        zh2, c2, zl2, y2, x2 = fn(zh, c, zl, y, x)
        out.append((i, (zh2 * 2 + c2) * 32 + zl2 * 16 + (y2 % 4) * 4 + x2 % 4))
    return out


def move(value, fn):
    return lax.ppermute(value, BOTH, pairs(fn))


def other_core(zh, c, zl, y, x):
    return (zh, 1 - c, zl, y, x)


def other_zh(zh, c, zl, y, x):
    return (1 - zh, c, zl, y, x)


def other_zl(zh, c, zl, y, x):
    return (zh, c, 1 - zl, y, x)


def first_axis(k):
    return lambda zh, c, zl, y, x: (zh, c, zl, y + (k if c else 0), x + (0 if c else k))


def second_axis(k):
    return lambda zh, c, zl, y, x: (zh, c, zl, y + (0 if c else k), x + (k if c else 0))


SHIFTS = (0, 1, 3, 2)


def place():
    p = lax.axis_index("pipe")
    return p // 2, p % 2


def to_rows(value):
    return jnp.sum(jnp.transpose(value), axis=0, keepdims=True)


def to_cols(row):
    return jnp.transpose(jnp.broadcast_to(row, (M, H)))


def extra_rows(row):
    high = row.astype(BF16)
    low = (row - high.astype(F32)).astype(BF16)
    i = lax.broadcasted_iota(jnp.int32, (16, M), 0)
    value = jnp.where(i == 0, high.astype(F32), jnp.where(i == 1, low.astype(F32), 0.0))
    return value.astype(BF16)


def read_extra(block):
    return jnp.sum(block.astype(F32), axis=0, keepdims=True)


def weight_copies(tick, w_ref, r_ref, buf, sem, start):
    zh, c = place()
    copy_index = zh if tick < 2 else 1 - zh
    e = zh ^ c
    own = (e == 0) if tick in (0, 3) else (e == 1)
    for ch in range(4):
        part = pl.ds(8 * ch, 8)
        received = pltpu.make_async_copy(r_ref.at[copy_index, part], buf.at[part], sem.at[ch])
        if start:

            @pl.when(own)
            def _():
                pltpu.make_async_copy(w_ref.at[copy_index, part, c], buf.at[part], sem.at[ch]).start()

            @pl.when(jnp.logical_not(own))
            def _():
                received.start()


def weight_wait(ch, w_ref, r_ref, buf, sem):
    part = pl.ds(8 * ch, 8)
    pltpu.make_async_copy(r_ref.at[0, part], buf.at[part], sem.at[ch]).wait()


def payload_kernel(x_ref, gain_ref, out_ref, f_ref):
    x = x_ref[...].astype(F32)
    f = (x * gain_ref[...].astype(F32)).astype(BF16)
    f_ref[...] = f
    extra = extra_rows(to_rows(x * x))
    for j in range(N):
        out_ref[j, 0:M, :] = f
        out_ref[j, M:R, :] = extra


def forward_kernel(tick, rows, g_ref, w_ref, r_ref, keep_ref, send_ref, buf, sem):
    weight_copies(tick, w_ref, r_ref, buf, sem, True)
    _, c = place()
    if rows == R:
        sums = jnp.sum(g_ref[:, M:R, :].astype(F32), axis=0)
        sums = jnp.sum(sums, axis=0, keepdims=True)
    else:
        sums = jnp.zeros((1, M), F32)
    sums = jnp.broadcast_to(sums, (8, M))
    total = jnp.zeros((M, 2 * H), F32)
    for ch in range(4):
        f = jnp.concatenate([g_ref[8 * ch + j, 0:M, :] for j in range(8)], axis=1)
        weight_wait(ch, w_ref, r_ref, buf, sem)
        w = buf[8 * ch : 8 * ch + 8].reshape(8 * 128, 2 * H)
        total = total + jnp.dot(f, w, preferred_element_type=F32)
    first = c == 0
    keep_ref[0:M, :] = jnp.where(first, total[:, :H], total[:, H:])
    send_ref[0:M, :] = jnp.where(first, total[:, H:], total[:, :H])
    keep_ref[M : M + 8, :] = sums
    send_ref[M : M + 8, :] = sums


def combine_kernel(keep_ref, recv_ref, x_ref, gain_ref, next_ref, p_ref, s_ref, out_ref=None, f_ref=None):
    squares = keep_ref[M : M + 8, :] + recv_ref[M : M + 8, :]
    scale = lax.rsqrt(squares / D + EPS)
    s_ref[...] = scale
    p = keep_ref[0:M, :] + recv_ref[0:M, :]
    p_ref[...] = p
    new = (x_ref[...].astype(F32) + to_cols(scale[0:1]) * p).astype(BF16)
    next_ref[...] = new
    if out_ref is not None:
        x = new.astype(F32)
        f = (x * gain_ref[...].astype(F32)).astype(BF16)
        f_ref[...] = f
        extra = extra_rows(to_rows(x * x))
        for j in range(N):
            out_ref[j, 0:M, :] = f
            out_ref[j, M:R, :] = extra


def last_combine_kernel(keep_ref, recv_ref, x_ref, s_ref, next_ref):
    p = keep_ref[0:M, :] + recv_ref[0:M, :]
    next_ref[...] = (x_ref[...].astype(F32) + to_cols(s_ref[0:1, :]) * p).astype(BF16)


def backward_kernel(tick, mine_ref, theirs_ref, s_ref, w_ref, r_ref, out_ref, gs_ref, buf, sem):
    weight_copies(tick, w_ref, r_ref, buf, sem, True)
    _, c = place()
    first = c == 0
    a = mine_ref[0:M, :]
    b = theirs_ref[0:M, :]
    left = jnp.where(first, a, b).astype(F32)
    right = jnp.where(first, b, a).astype(F32)
    scale = to_cols(s_ref[0:1, :])
    gs_ref[:, :H] = (left * scale).astype(BF16)
    gs_ref[:, H:] = (right * scale).astype(BF16)
    extra = extra_rows(read_extra(mine_ref[M:R, :]) + read_extra(theirs_ref[M:R, :]))
    gt = jnp.concatenate([jnp.transpose(left), jnp.transpose(right)], axis=0).astype(BF16)
    for ch in range(4):
        weight_wait(ch, w_ref, r_ref, buf, sem)
        w = buf[8 * ch : 8 * ch + 8].reshape(8 * 128, 2 * H)
        part = jnp.dot(w, gt, preferred_element_type=F32).astype(BF16).reshape(8, 128, M)
        out_ref[8 * ch : 8 * ch + 8, 0:M, :] = part
    for j in range(N):
        out_ref[j, M:R, :] = extra


def first_backward_kernel(g_ref, w_ref, r_ref, out_ref, buf, sem):
    weight_copies(3, w_ref, r_ref, buf, sem, True)
    g = g_ref[...].astype(F32)
    gt = jnp.concatenate([jnp.transpose(g[:, :H]), jnp.transpose(g[:, H:])], axis=0).astype(BF16)
    for ch in range(4):
        weight_wait(ch, w_ref, r_ref, buf, sem)
        w = buf[8 * ch : 8 * ch + 8].reshape(8 * 128, 2 * H)
        out_ref[8 * ch : 8 * ch + 8] = jnp.dot(w, gt, preferred_element_type=F32).astype(BF16).reshape(8, 128, M)


def sum_kernel(got_ref, gain_ref, gn_ref):
    total = jnp.sum(got_ref[...].astype(F32), axis=0)
    gn_ref[...] = jnp.transpose(total) * gain_ref[...].astype(F32)


def scalars_kernel(x_ref, gn_ref, out_ref):
    x = x_ref[...].astype(F32)
    i = lax.broadcasted_iota(jnp.int32, (8, M), 0)
    out_ref[...] = jnp.where(i == 0, to_rows(x * x), jnp.where(i == 1, to_rows(x * gn_ref[...]), 0.0))


def spread_kernel(a_ref, b_ref, out_ref):
    total = a_ref[...] + b_ref[...]
    for j in range(N):
        out_ref[j] = total


def last_grad_kernel(sums_ref, g_ref, gn_ref, x_ref, p_ref, out_ref, s_ref):
    total = jnp.sum(sums_ref[...], axis=0)
    scale = lax.rsqrt(total[0:1, :] / D + EPS)
    s_ref[...] = jnp.broadcast_to(scale, (8, M))
    mix = scale * scale * scale * total[1:2, :] / D
    g = g_ref[...].astype(F32) + to_cols(scale) * gn_ref[...] - to_cols(mix) * x_ref[...].astype(F32)
    g = g.astype(BF16)
    out_ref[0:M, :] = g
    out_ref[M:R, :] = extra_rows(to_rows(g.astype(F32) * p_ref[...]))


def grad_kernel(got_ref, gain_ref, g_ref, s_ref, x_ref, out_ref):
    total = jnp.sum(got_ref[:, 0:M, :].astype(F32), axis=0)
    dots = jnp.sum(jnp.sum(got_ref[:, M:R, :].astype(F32), axis=0), axis=0, keepdims=True)
    gn = jnp.transpose(total) * gain_ref[...].astype(F32)
    scale = s_ref[0:1, :]
    mix = scale * scale * scale * dots / D
    g = g_ref[0:M, :].astype(F32) + to_cols(scale) * gn - to_cols(mix) * x_ref[...].astype(F32)
    out_ref[...] = g.astype(BF16)


def dots_kernel(g_ref, p_ref, out_ref):
    g = g_ref[...]
    out_ref[0:M, :] = g
    out_ref[M:R, :] = extra_rows(to_rows(g.astype(F32) * p_ref[...]))


def order_kernel(v0, v1, v2, v3, f0, f1, f2, f3_ref, keep_ref, send_ref):
    zh, c = place()
    dp = lax.axis_index("dp")
    zl, y, x = dp // 16, (dp // 4) % 4, dp % 4
    a0 = jnp.where(c == 0, x, y)
    b0 = jnp.where(c == 0, y, x)
    sa = jnp.where(c == 0, 1, 4)
    sb = jnp.where(c == 0, 4, 1)
    second = c == 1

    def turn(v):
        return jnp.transpose(v.astype(F32)).astype(BF16)

    def put(j, q, down, up):
        pair = jnp.concatenate([turn(down), turn(up)], axis=1)

        @pl.when(c == q)
        def _():
            keep_ref[j] = pair

        @pl.when(c != q)
        def _():
            send_ref[j] = pair

    for ib, kb in enumerate(SHIFTS):
        ref = (v0, v1, v2, v3)[ib]
        jb = lax.rem(b0 + 4 - kb, 4) * sb
        for ia, ka in enumerate(SHIFTS):
            ja = lax.rem(a0 + 4 - ka, 4) * sa
            for iz in range(2):
                j = jb + ja + (zl if iz == 0 else 1 - zl) * 16
                at = ia * 2 + iz
                last = ref[at, 0]
                f3_ref[j] = last
                d0 = jnp.where(zh == 0, f0[j, 0:M, :], f2[j, 0:M, :])
                d1 = jnp.where(zh == 0, f1[j, 0:M, :], last)
                put(j, 0, d0, ref[at, 1])
                put(j, 1, d1, ref[at, 2])


def weight_grad_kernel(keep_ref, recv_ref, local_ref, far_ref, factor_ref, out_ref):
    _, c = place()
    g = jnp.concatenate([local_ref[...], far_ref[...]], axis=0)
    count = keep_ref.shape[0]
    a = jnp.dot(keep_ref[...].reshape(count * H, 2 * M), g, preferred_element_type=F32).reshape(count, H, 2 * H)
    b = jnp.dot(recv_ref[...].reshape(count * H, 2 * M), g, preferred_element_type=F32).reshape(count, H, 2 * H)
    first = c == 0
    out_ref[:, 0] = (jnp.where(first, a, b) * factor_ref[:, 0]).astype(BF16)
    out_ref[:, 1] = (jnp.where(first, b, a) * factor_ref[:, 1]).astype(BF16)


def call(kernel, out, specs, args, scratch=(), flops=0, bytes_accessed=0):
    return pl.pallas_call(
        kernel,
        out_shape=[jax.ShapeDtypeStruct(s, d) for s, d in out],
        in_specs=specs,
        out_specs=[VM] * len(out),
        scratch_shapes=list(scratch),
        compiler_params=PARAMS,
        cost_estimate=pl.CostEstimate(flops=flops, bytes_accessed=bytes_accessed, transcendentals=0),
    )(*args)


WEIGHT_SCRATCH = (pltpu.VMEM((N, H, 2 * H), BF16), pltpu.SemaphoreType.DMA((4,)))
MATMUL = dict(scratch=WEIGHT_SCRATCH, flops=2 * M * N * H * 2 * H, bytes_accessed=4 << 20)


def blocks_of(payload):
    return lax.all_to_all(payload, "dp", 0, 0)


def gather_relative(value):
    both = jnp.stack([value, move(value, other_zl)])
    row = jnp.concatenate([both] + [move(both, first_axis(k)) for k in SHIFTS[1:]])
    return [row] + [move(row, second_axis(k)) for k in SHIFTS[1:]]


def on_device(batches, cotangents, weights, gains, exponents):
    zh, c = place()
    e = zh ^ c
    w5 = weights.reshape(2, N, 2, H, 2 * H)

    def half(value, which):
        return lax.dynamic_slice_in_dim(value, which * H, H, axis=value.ndim - 1)

    own_gain = half(gains[:, 0], c)
    got_gain = move(half(gains[:, 0], 1 - c), other_core)
    gain = []
    for tick in range(4):
        copy_index = zh if tick < 2 else 1 - zh
        own = (e == 0) if tick in (0, 3) else (e == 1)
        both = jnp.where(own, own_gain, got_gain)
        gain.append(lax.dynamic_slice_in_dim(both, copy_index, 1, axis=0))

    send_w = lax.dynamic_index_in_dim(w5, 1 - c, axis=2, keepdims=False)
    r_w = move(send_w, other_core)

    x0 = half(lax.dynamic_index_in_dim(batches, zh, axis=0, keepdims=False), c)
    block = (M, H)
    wide = ((N, R, H), BF16)
    out0, f0 = call(payload_kernel, [wide, (block, BF16)], [VM] * 2, (x0, gain[0]))
    g0 = blocks_of(out0)

    def forward(tick, gathered):
        keep, send = call(
            functools.partial(forward_kernel, tick, gathered.shape[1]),
            [((M + 8, H), F32)] * 2,
            [VM, HBM, HBM],
            (gathered, w5, r_w),
            **MATMUL,
        )
        return keep, move(send, other_core)

    outs = [(block, BF16), (block, F32), ((8, M), F32)]
    keep, recv = forward(0, g0)
    x1, _, s0, out1, f1 = call(
        combine_kernel, outs + [wide, (block, BF16)], [VM] * 4, (keep, recv, x0, gain[1])
    )
    g1 = blocks_of(out1)
    keep, recv = forward(1, g1)
    x2, p1, s1 = call(combine_kernel, outs, [VM] * 4, (keep, recv, x1, gain[1]))
    x2 = move(x2, other_zh)
    out2, f2 = call(payload_kernel, [wide, (block, BF16)], [VM] * 2, (x2, gain[2]))
    g2 = blocks_of(out2)

    cot = lax.dynamic_index_in_dim(cotangents, 1 - zh, axis=0, keepdims=False)
    (part,) = call(
        first_backward_kernel, [((N, H, M), BF16)], [VM, HBM, HBM], (cot, w5, r_w), **MATMUL
    )
    (gn3,) = call(sum_kernel, [(block, F32)], [VM] * 2, (blocks_of(part), gain[3]))

    keep, recv = forward(2, g2)
    x3, p2, s2, _, f3 = call(
        combine_kernel, outs + [wide, (block, BF16)], [VM] * 4, (keep, recv, x2, gain[3])
    )

    (mine,) = call(scalars_kernel, [((8, M), F32)], [VM] * 2, (x3, gn3))
    theirs = move(mine, other_core)
    (spread,) = call(spread_kernel, [((N, 8, M), F32)], [VM] * 2, (mine, theirs))
    sums = blocks_of(spread)

    early = jnp.stack([f0, f1])
    late = jnp.stack([f2, f3])
    mirror = move(jnp.where(zh == 1, early, late), other_zh)
    v = gather_relative(jnp.concatenate([f3[None], mirror]))

    g3 = half(cot, c)
    mine2, s3 = call(
        last_grad_kernel, [((R, H), BF16), ((8, M), F32)], [VM] * 5, (sums, g3, gn3, x3, p2)
    )

    def backward(tick, mine, s):
        theirs = move(mine, other_core)
        part, gs = call(
            functools.partial(backward_kernel, tick),
            [wide, ((M, 2 * H), BF16)],
            [VM] * 3 + [HBM] * 2,
            (mine, theirs, s, w5, r_w),
            **MATMUL,
        )
        return blocks_of(part), gs

    got2, gs2 = backward(2, mine2, s2)
    (g1_,) = call(grad_kernel, [(block, BF16)], [VM] * 5, (got2, gain[2], mine2, s2, x2))
    g1_ = move(g1_, other_zh)
    (mine1,) = call(dots_kernel, [((R, H), BF16)], [VM] * 2, (g1_, p1))
    got1, gs1 = backward(1, mine1, s1)
    (g0_,) = call(grad_kernel, [(block, BF16)], [VM] * 5, (got1, gain[1], mine1, s1, x1))

    f3_all, keep_t, send_t = call(
        order_kernel,
        [((N, M, H), BF16), ((N, H, 2 * M), BF16), ((N, H, 2 * M), BF16)],
        [VM] * 7,
        (*v, g0, g1, g2),
    )
    recv_t = move(send_t, other_core)
    keep, recv = forward(3, f3_all)
    (x4,) = call(last_combine_kernel, [(block, BF16)], [VM] * 4, (keep, recv, x3, s3))
    is_first = e == 0
    shown = jnp.where(is_first, x4, x3)
    got = move(jnp.where(is_first, x3, x4), other_core)
    last = jnp.where(c == 0, jnp.concatenate([shown, got], 1), jnp.concatenate([got, shown], 1))

    def scaled(g, s):
        return (g.astype(F32) * s[0][:, None]).astype(BF16)

    mine0 = scaled(g0_, s0)
    theirs0 = move(mine0, other_core)
    gs0 = jnp.where(c == 0, jnp.concatenate([mine0, theirs0], 1), jnp.concatenate([theirs0, mine0], 1))
    gs3 = scaled(cot, s3)
    low = jnp.where(c == 0, gs0, gs1)
    high = jnp.where(c == 0, gs2, gs3)
    local = jnp.where(zh == 0, low, high)
    far = move(jnp.where(zh == 0, high, low), other_zh)
    factor = jnp.repeat(jnp.exp2(-exponents[0].astype(F32)), H, axis=1).reshape(N, 2, 1, 2 * H)
    step = 8
    total = pl.pallas_call(
        weight_grad_kernel,
        out_shape=jax.ShapeDtypeStruct((N, 2, H, 2 * H), BF16),
        grid=(N // step,),
        in_specs=[
            pl.BlockSpec((step, H, 2 * M), lambda i: (i, 0, 0)),
            pl.BlockSpec((step, H, 2 * M), lambda i: (i, 0, 0)),
            pl.BlockSpec((M, 2 * H), lambda i: (0, 0)),
            pl.BlockSpec((M, 2 * H), lambda i: (0, 0)),
            pl.BlockSpec((step, 2, 1, 2 * H), lambda i: (i, 0, 0, 0)),
        ],
        out_specs=pl.BlockSpec((step, 2, H, 2 * H), lambda i: (i, 0, 0, 0)),
        compiler_params=PARAMS,
        cost_estimate=pl.CostEstimate(flops=2 * 256 * 256 * D, bytes_accessed=8 << 20, transcendentals=0),
    )(keep_t, recv_t, local, far, factor)
    return (total.reshape(1, D, 2 * H), last[None])


def solution(mesh):
    return jax.shard_map(
        on_device,
        mesh=mesh,
        in_specs=(
            P(None, None, "dp"),
            P(None, None, "dp"),
            P(None, "pipe", None, "dp"),
            P(None, "pipe", "dp"),
            P("pipe", None, "dp"),
        ),
        out_specs=(P("pipe", None, "dp"), P("pipe", None, "dp")),
        check_vma=False,
    )
```

```python
import functools

import jax
import jax.numpy as jnp
from jax import lax
from jax.experimental import pallas as pl
from jax.experimental.pallas import tpu as pltpu
from jax.sharding import PartitionSpec as P

D = 8192
EPS = 1e-05
M = 128
H = 128
N = 32
R = M + 16
F32 = jnp.float32
BF16 = jnp.bfloat16
BOTH = ("pipe", "dp")
VM = pl.BlockSpec(memory_space=pltpu.VMEM)
HBM = pl.BlockSpec(memory_space=pltpu.HBM)
MIB = 1 << 20


def pairs(fn):
    out = []
    for i in range(128):
        p, d = divmod(i, 32)
        zh, c = divmod(p, 2)
        zl, r = divmod(d, 16)
        y, x = divmod(r, 4)
        zh2, c2, zl2, y2, x2 = fn(zh, c, zl, y, x)
        out.append((i, (zh2 * 2 + c2) * 32 + zl2 * 16 + (y2 % 4) * 4 + x2 % 4))
    return out


def move(value, fn):
    return lax.ppermute(value, BOTH, pairs(fn))


def move_some(value, fn, keep):
    return lax.ppermute(value, BOTH, [(i, j) for i, j in pairs(fn) if (i // 64, i // 32 % 2) in keep])


def other_core(zh, c, zl, y, x):
    return (zh, 1 - c, zl, y, x)


def other_zh(zh, c, zl, y, x):
    return (1 - zh, c, zl, y, x)


def other_both(zh, c, zl, y, x):
    return (1 - zh, 1 - c, zl, y, x)


def other_zl(zh, c, zl, y, x):
    return (zh, c, 1 - zl, y, x)


def first_axis(k):
    return lambda zh, c, zl, y, x: (zh, c, zl, y + (k if c else 0), x + (0 if c else k))


def second_axis(k):
    return lambda zh, c, zl, y, x: (zh, c, zl, y + (0 if c else k), x + (k if c else 0))


def along_y(k):
    return lambda zh, c, zl, y, x: (zh, c, zl, y + k, x)


SHIFTS = (0, 1, 3, 2)


def place():
    p = lax.axis_index("pipe")
    return p // 2, p % 2


def block_index(sign):
    _, c = place()
    dp = lax.axis_index("dp")
    y, x = (dp // 4) % 4, dp % 4
    b = jnp.where(c == 0, y, x)
    sa = jnp.where(c == 0, 1, 4)
    sb = jnp.where(c == 0, 4, 1)

    def index(ib, i):
        return lax.rem(b + 4 + sign * SHIFTS[ib], 4) * sb + (i % 4) * sa + (i // 4) * 16

    return index


def step_index():
    _, c = place()
    dp = lax.axis_index("dp")
    zl, y, x = dp // 16, (dp // 4) % 4, dp % 4
    a = jnp.where(c == 0, x, y)
    b = jnp.where(c == 0, y, x)
    sa = jnp.where(c == 0, 1, 4)
    sb = jnp.where(c == 0, 4, 1)

    def index(ib, ia, iz):
        jb = lax.rem(b + 4 - SHIFTS[ib], 4) * sb
        ja = lax.rem(a + 4 - SHIFTS[ia], 4) * sa
        return jb + ja + (zl if iz == 0 else 1 - zl) * 16

    return index


def to_rows(value):
    return jnp.sum(jnp.transpose(value), axis=0, keepdims=True)


def to_cols(row):
    return jnp.transpose(jnp.broadcast_to(row, (M, H)))


def extra_rows(row):
    high = row.astype(BF16)
    low = (row - high.astype(F32)).astype(BF16)
    i = lax.broadcasted_iota(jnp.int32, (16, M), 0)
    value = jnp.where(i == 0, high.astype(F32), jnp.where(i == 1, low.astype(F32), 0.0))
    return value.astype(BF16)


def read_extra(block):
    return jnp.sum(block.astype(F32), axis=0, keepdims=True)


def split_kernel(w_ref, own_ref, send_ref, sem):
    _, c = place()
    copies = [pltpu.make_async_copy(w_ref.at[b, :, 1 - c], send_ref.at[b], sem.at[b]) for b in range(2)]
    copies += [pltpu.make_async_copy(w_ref.at[b, :, c], own_ref.at[b], sem.at[2 + b]) for b in range(2)]
    for copy in copies:
        copy.start()
    for copy in copies:
        copy.wait()


def pick_kernel(own_ref, other_ref, out_ref, sem):
    zh, c = place()

    def run(own_ticks, other_ticks):
        copies = []
        for i in range(2):
            b = zh if i == 0 else 1 - zh
            copies.append(pltpu.make_async_copy(own_ref.at[b], out_ref.at[own_ticks[i]], sem.at[i]))
            copies.append(pltpu.make_async_copy(other_ref.at[b], out_ref.at[other_ticks[i]], sem.at[2 + i]))
        for copy in copies:
            copy.start()
        for copy in copies:
            copy.wait()

    pl.when((zh ^ c) == 0)(lambda: run((0, 3), (1, 2)))
    pl.when((zh ^ c) == 1)(lambda: run((1, 2), (0, 3)))


def load_kernel(tick, w_ref, out_ref, sem):
    parts = [pl.ds(N // 8 * i, N // 8) for i in range(8)]
    copies = [pltpu.make_async_copy(w_ref.at[tick, q], out_ref.at[q], sem.at[i]) for i, q in enumerate(parts)]
    for copy in copies:
        copy.start()
    for copy in copies:
        copy.wait()


def payload_kernel(x_ref, gain_ref, out_ref, ft_ref):
    x = x_ref[...].astype(F32)
    f = (x * gain_ref[...].astype(F32)).astype(BF16)
    ft_ref[...] = jnp.transpose(f)
    extra = extra_rows(to_rows(x * x))
    for j in range(out_ref.shape[0]):
        out_ref[j, 0:M, :] = f
        out_ref[j, M:R, :] = extra


def forward_kernel(v0, v1, v2, v3, w_ref, keep_ref, send_ref):
    _, c = place()
    index = block_index(-1)
    sums = jnp.zeros((16, M), F32)
    total = jnp.zeros((M, 2 * H), F32)
    for ref in (v0, v1, v2, v3):
        sums = sums + jnp.sum(ref[:, M:R, :].astype(F32), axis=0)
    for ib, ref in enumerate((v0, v1, v2, v3)):
        f = jnp.concatenate([ref[i, 0:M, :] for i in range(8)], axis=1)
        w = jnp.concatenate([w_ref[index(ib, i)] for i in range(8)], axis=0)
        total = total + jnp.dot(f, w, preferred_element_type=F32)
    sums = jnp.broadcast_to(jnp.sum(sums, axis=0, keepdims=True), (8, M))
    first = c == 0
    keep_ref[0:M, :] = jnp.where(first, total[:, :H], total[:, H:])
    send_ref[0:M, :] = jnp.where(first, total[:, H:], total[:, :H])
    keep_ref[M : M + 8, :] = sums
    send_ref[M : M + 8, :] = sums


def last_forward_kernel(f_ref, w_ref, keep_ref, send_ref):
    _, c = place()
    total = jnp.zeros((M, 2 * H), F32)
    for ch in range(4):
        f = jnp.concatenate([f_ref[8 * ch + j] for j in range(8)], axis=1)
        w = w_ref[8 * ch : 8 * ch + 8].reshape(8 * 128, 2 * H)
        total = total + jnp.dot(f, w, preferred_element_type=F32)
    first = c == 0
    keep_ref[...] = jnp.where(first, total[:, :H], total[:, H:])
    send_ref[...] = jnp.where(first, total[:, H:], total[:, :H])


def combine_kernel(keep_ref, recv_ref, x_ref, gain_ref, next_ref, p_ref, s_ref, out_ref=None, ft_ref=None):
    squares = keep_ref[M : M + 8, :] + recv_ref[M : M + 8, :]
    scale = lax.rsqrt(squares / D + EPS)
    s_ref[...] = scale
    p = keep_ref[0:M, :] + recv_ref[0:M, :]
    p_ref[...] = p
    new = (x_ref[...].astype(F32) + to_cols(scale[0:1]) * p).astype(BF16)
    next_ref[...] = new
    if out_ref is not None:
        x = new.astype(F32)
        f = (x * gain_ref[...].astype(F32)).astype(BF16)
        ft_ref[...] = jnp.transpose(f)
        extra = extra_rows(to_rows(x * x))
        for j in range(out_ref.shape[0]):
            out_ref[j, 0:M, :] = f
            out_ref[j, M:R, :] = extra


def third_combine_kernel(keep_ref, recv_ref, x_ref, gain_ref, gn_ref, next_ref, p_ref, s_ref, f_ref, ft_ref, sums_ref):
    squares = keep_ref[M : M + 8, :] + recv_ref[M : M + 8, :]
    scale = lax.rsqrt(squares / D + EPS)
    s_ref[...] = scale
    p = keep_ref[0:M, :] + recv_ref[0:M, :]
    p_ref[...] = p
    new = (x_ref[...].astype(F32) + to_cols(scale[0:1]) * p).astype(BF16)
    next_ref[...] = new
    x = new.astype(F32)
    f = (x * gain_ref[...].astype(F32)).astype(BF16)
    f_ref[...] = f
    ft_ref[...] = jnp.transpose(f)
    i = lax.broadcasted_iota(jnp.int32, (8, M), 0)
    sums = jnp.where(i == 0, to_rows(x * x), jnp.where(i == 1, to_rows(x * gn_ref[...]), 0.0))
    for j in range(16):
        sums_ref[j] = sums


def last_combine_kernel(keep_ref, recv_ref, x_ref, s_ref, next_ref):
    p = keep_ref[...] + recv_ref[...]
    next_ref[...] = (x_ref[...].astype(F32) + to_cols(s_ref[0:1, :]) * p).astype(BF16)


def turned(left, right):
    return jnp.concatenate([jnp.transpose(left), jnp.transpose(right)], axis=0)


def backward_kernel(mine_ref, theirs_ref, s_ref, w_ref, o0, o1, o2, o3, gs_ref):
    _, c = place()
    first = c == 0
    a = mine_ref[0:M, :]
    b = theirs_ref[0:M, :]
    left = jnp.where(first, a, b)
    right = jnp.where(first, b, a)
    scale = to_cols(s_ref[0:1, :])
    gs_ref[:, :H] = (left.astype(F32) * scale).astype(BF16)
    gs_ref[:, H:] = (right.astype(F32) * scale).astype(BF16)
    extra = extra_rows(read_extra(mine_ref[M:R, :]) + read_extra(theirs_ref[M:R, :]))
    gt = turned(left, right)
    index = block_index(1)
    for ib, ref in enumerate((o0, o1, o2, o3)):
        w = jnp.concatenate([w_ref[index(ib, i)] for i in range(8)], axis=0)
        ref[:, 0:M, :] = jnp.dot(w, gt, preferred_element_type=F32).astype(BF16).reshape(8, H, M)
        for i in range(8):
            ref[i, M:R, :] = extra


def first_backward_kernel(g_ref, w_ref, o0, o1, o2, o3):
    gt = turned(g_ref[:, :H], g_ref[:, H:])
    index = block_index(1)
    for ib, ref in enumerate((o0, o1, o2, o3)):
        w = jnp.concatenate([w_ref[index(ib, i)] for i in range(8)], axis=0)
        ref[...] = jnp.dot(w, gt, preferred_element_type=F32).astype(BF16).reshape(8, H, M)


def sum_kernel(r0, r1, r2, r3, out):
    total = r0[...].astype(F32) + r1[...].astype(F32) + r2[...].astype(F32) + r3[...].astype(F32)
    out[:, 0:M, :] = total[:, 0:M, :].astype(BF16)
    if total.shape[1] == R:
        for i in range(8):
            out[i, M:R, :] = extra_rows(jnp.sum(total[i, M:R, :], axis=0, keepdims=True))


def last_sum_kernel(got_ref, gain_ref, gn_ref):
    total = jnp.sum(got_ref[...].astype(F32), axis=0)
    gn_ref[...] = jnp.transpose(total) * gain_ref[...].astype(F32)


def choose_kernel(a_ref, b_ref, out):
    zh, _ = place()
    out[...] = jnp.where(zh == 0, a_ref[...], b_ref[...])


def join_kernel(r0, r1, r2, r3, out):
    n = r0.shape[0]
    for i, ref in enumerate((r0, r1, r2, r3)):
        out[i * n : (i + 1) * n] = ref[...]


def turned(left, right):
    return jnp.concatenate([jnp.transpose(left), jnp.transpose(right)], axis=0)


def add_kernel(r, out):
    out[...] = jnp.sum(r[...], axis=0)


def last_grad_kernel(s0, s1, s2, s3, g_ref, gn_ref, x_ref, p_ref, out_ref, s_ref):
    total = s0[...] + s1[...] + s2[...] + s3[...]
    scale = lax.rsqrt(total[0:1, :] / D + EPS)
    s_ref[...] = jnp.broadcast_to(scale, (8, M))
    mix = scale * scale * scale * total[1:2, :] / D
    g = g_ref[...].astype(F32) + to_cols(scale) * gn_ref[...] - to_cols(mix) * x_ref[...].astype(F32)
    g = g.astype(BF16)
    out_ref[0:M, :] = g
    out_ref[M:R, :] = extra_rows(to_rows(g.astype(F32) * p_ref[...]))


def grad_kernel(got_ref, gain_ref, g_ref, s_ref, x_ref, *rest):
    out_ref = rest[-1]
    total = jnp.sum(got_ref[:, 0:M, :].astype(F32), axis=0)
    dots = jnp.sum(jnp.sum(got_ref[:, M:R, :].astype(F32), axis=0), axis=0, keepdims=True)
    gn = jnp.transpose(total) * gain_ref[...].astype(F32)
    scale = s_ref[0:1, :]
    mix = scale * scale * scale * dots / D
    g = g_ref[0:M, :].astype(F32) + to_cols(scale) * gn - to_cols(mix) * x_ref[...].astype(F32)
    if len(rest) == 2:
        g = g.astype(BF16).astype(F32) * to_cols(rest[0][0:1, :])
    out_ref[...] = g.astype(BF16)


def dots_kernel(g_ref, p_ref, out_ref):
    g = g_ref[...]
    out_ref[0:M, :] = g
    out_ref[M:R, :] = extra_rows(to_rows(g.astype(F32) * p_ref[...]))


def order_kernel(*refs):
    v, g0, g1, g2 = refs[0:4], refs[4:8], refs[8:12], refs[12:16]
    f3_ref, keep_ref, send_ref = refs[16:]
    zh, c = place()
    index = step_index()
    other = block_index(-1)

    def fill(first, second, q0_ref, q1_ref):
        for ib in range(4):
            for ia in range(4):
                for iz in range(2):
                    j = index(ib, ia, iz)
                    at = ia * 2 + iz
                    last = v[ib][at, 0]
                    f3_ref[j] = last
                    q0_ref[j, :, M:] = v[ib][at, 1]
                    q1_ref[j, :, M:] = v[ib][at, 2]
                    if second is None:
                        q1_ref[j, :, :M] = jnp.transpose(last)
            for i in range(8):
                j = other(ib, i)
                q0_ref[j, :, :M] = jnp.transpose(first[ib][i, 0:M, :])
                if second is not None:
                    q1_ref[j, :, :M] = jnp.transpose(second[ib][i, 0:M, :])

    for a in range(2):
        for b in range(2):
            q0, q1 = (keep_ref, send_ref) if b == 0 else (send_ref, keep_ref)
            first, second = (g0, g1) if a == 0 else (g2, None)
            pl.when(jnp.logical_and(zh == a, c == b))(functools.partial(fill, first, second, q0, q1))


def weight_grad_kernel(
    keep_ref, recv_ref, local_ref, far_ref, mine_ref, core_ref, far0_ref, far1_ref, factor_ref, out_ref, buf, sem
):
    zh, c = place()
    late = (zh + c) == 0
    local = jnp.where(late, jnp.concatenate([mine_ref[...], core_ref[...]], axis=1), local_ref[...])
    far = jnp.where(late, jnp.concatenate([far0_ref[...], far1_ref[...]], axis=1), far_ref[...])
    g = jnp.concatenate([local, far], axis=0)
    count = 4
    copies = []
    for i in range(N // count):
        part = pl.ds(i * count, count)
        for ref, which in ((keep_ref, c), (recv_ref, 1 - c)):
            value = jnp.dot(ref[part].reshape(count * H, 2 * M), g, preferred_element_type=F32)
            value = value.reshape(count, H, 2 * H) * factor_ref[part, which]
            buf[part, which] = value.astype(BF16)
        copies.append(pltpu.make_async_copy(buf.at[part], out_ref.at[part], sem.at[i]))
        copies[-1].start()
    for copy in copies:
        copy.wait()


def call(kernel, out, specs, args, scratch=(), flops=0, bytes_accessed=0, limit=4, out_specs=None, deps=()):
    count = len(args)

    def body(*refs):
        kernel(*refs[:count], *refs[count + len(deps) :])

    return pl.pallas_call(
        body,
        out_shape=[jax.ShapeDtypeStruct(s, d) for s, d in out],
        in_specs=list(specs) + [pl.BlockSpec(memory_space=pl.ANY)] * len(deps),
        out_specs=out_specs or [VM] * len(out),
        scratch_shapes=list(scratch),
        compiler_params=pltpu.CompilerParams(vmem_limit_bytes=limit * MIB),
        cost_estimate=pl.CostEstimate(flops=flops, bytes_accessed=bytes_accessed, transcendentals=0),
    )(*args, *deps)


MATMUL = dict(
    flops=2 * M * N * H * 2 * H,
    bytes_accessed=4 << 20,
    limit=6,
)


def plane_groups():
    groups = {}
    for i in range(128):
        p, d = divmod(i, 32)
        c = p % 2
        y, x = (d // 4) % 4, d % 4
        groups.setdefault((p, y if c == 0 else x), []).append((d // 16, x if c == 0 else y, i))
    return [[i for _, _, i in sorted(g)] for g in groups.values()]


PLANES = plane_groups()


def core_groups():
    groups = {}
    for i in range(128):
        p, d = divmod(i, 32)
        groups.setdefault((p // 2, (d // 4) % 4), []).append(i)
    return list(groups.values())


CORES = core_groups()


def exchange(value):
    return lax.all_to_all(value, BOTH, 0, 0, axis_index_groups=PLANES)


def along_second(parts):
    return [parts[0]] + [move(parts[i], second_axis(SHIFTS[i])) for i in (1, 2, 3)]


def gather(payload):
    row = exchange(payload)
    return along_second([row] * 4)


def scatter(parts, *deps):
    shape = parts[0].shape
    (total,) = call(sum_kernel, [(shape, BF16)], [VM] * 4, along_second(parts), deps=deps)
    return exchange(total), total


def gather_z(value):
    return jnp.stack([value, move(value, other_zl)])


def gather_first(both, dep):
    rows = [both] + [move(both, first_axis(k)) for k in SHIFTS[1:]]
    return call(join_kernel, [((8,) + both.shape[1:], BF16)], [VM] * 4, rows, deps=(dep,))[0]


def on_device(batches, cotangents, weights, gains, exponents):
    zh, c = place()
    e = zh ^ c
    w5 = weights.reshape(2, N, 2, H, 2 * H)

    def half(value, which):
        return lax.dynamic_slice_in_dim(value, which * H, H, axis=value.ndim - 1)

    own_gain = half(gains[:, 0], c)
    got_gain = move(half(gains[:, 0], 1 - c), other_core)
    gain = []
    for tick in range(4):
        copy_index = zh if tick < 2 else 1 - zh
        own = (e == 0) if tick in (0, 3) else (e == 1)
        both = jnp.where(own, own_gain, got_gain)
        gain.append(lax.dynamic_slice_in_dim(both, copy_index, 1, axis=0))

    x0 = half(lax.dynamic_index_in_dim(batches, zh, axis=0, keepdims=False), c)
    block = (M, H)
    wide = ((8, R, H), BF16)
    out0, ft0 = call(payload_kernel, [wide, (block, BF16)], [VM] * 2, (x0, gain[0]))
    g0 = gather(out0)

    started = move(ft0, other_core)
    own_w, send_w = call(
        split_kernel,
        [((2, N, H, 2 * H), BF16)] * 2,
        [VM],
        (w5,),
        scratch=[pltpu.SemaphoreType.DMA((4,))],
        out_specs=[HBM] * 2,
        limit=10,
        deps=(started,),
    )
    (all_w,) = call(
        pick_kernel,
        [((24, N, H, 2 * H), BF16)],
        [VM] * 2,
        (own_w, move(send_w, other_core)),
        scratch=[pltpu.SemaphoreType.DMA((4,))],
        out_specs=[HBM],
        limit=10,
    )

    def load(tick, *deps):
        return call(
            functools.partial(load_kernel, tick),
            [((N, H, 2 * H), BF16)],
            [HBM],
            (all_w,),
            scratch=[pltpu.SemaphoreType.DMA((8,))],
            deps=deps,
        )[0]

    cot = lax.dynamic_index_in_dim(cotangents, 1 - zh, axis=0, keepdims=False)
    first_parts = call(first_backward_kernel, [((8, H, M), BF16)] * 4, [VM] * 2, (cot, load(3)), **MATMUL)
    parts = along_second(first_parts)

    def forward(weight, gathered, deps):
        keep, send = call(
            forward_kernel, [((M + 8, H), F32)] * 2, [VM] * 5, (*gathered, weight), deps=deps, **MATMUL
        )
        return keep, move(send, other_core)

    outs = [(block, BF16), (block, F32), ((8, M), F32)]
    keep, recv = forward(load(0), g0, first_parts)
    x1, _, s0, out1, ft1 = call(
        combine_kernel, outs + [wide, (block, BF16)], [VM] * 4, (keep, recv, x0, gain[1])
    )
    g1 = gather(out1)
    (row3,) = call(sum_kernel, [((8, H, M), BF16)], [VM] * 4, parts)
    (gn3,) = call(last_sum_kernel, [(block, F32)], [VM] * 2, (exchange(row3), gain[3]))
    keep, recv = forward(load(1, out1), g1, ())
    x2, p1, s1 = call(combine_kernel, outs, [VM] * 4, (keep, recv, x1, gain[1]), deps=(gn3,))
    x2 = move(x2, other_zh)
    out2, ft2 = call(payload_kernel, [wide, (block, BF16)], [VM] * 2, (x2, gain[2]))
    g2 = gather(out2)
    mirror0 = move(jnp.where(zh == 1, ft0, ft2), other_zh)
    keep, recv = forward(load(2, out2), g2, (mirror0,))
    x3, p2, s2, f3, ft3, spread = call(
        third_combine_kernel,
        outs + [(block, BF16), (block, BF16), ((16, 8, M), F32)],
        [VM] * 5,
        (keep, recv, x2, gain[3], gn3),
    )
    (send3,) = call(choose_kernel, [(block, BF16)], [VM] * 2, (ft3, ft1), deps=(x3,))
    mirror1 = move(send3, other_zh)
    (sums,) = call(add_kernel, [((8, M), F32)], [VM], (lax.all_to_all(spread, BOTH, 0, 0, axis_index_groups=CORES),), deps=(mirror1,))
    first_rows = gather_z(jnp.stack([f3, mirror0, mirror1]))
    w2 = load(2, x3)
    sums = [sums] + [move(sums, along_y(k)) for k in SHIFTS[1:]]

    g3 = half(cot, c)
    mine2, s3 = call(
        last_grad_kernel,
        [((R, H), BF16), ((8, M), F32)],
        [VM] * 8,
        (*sums, g3, gn3, x3, p2),
        deps=(w2, first_rows),
    )

    def backward(weight, mine, s):
        theirs = move(mine, other_core)
        *parts, gs = call(
            backward_kernel, [wide] * 4 + [((M, 2 * H), BF16)], [VM] * 4, (mine, theirs, s, weight), **MATMUL
        )
        return parts, gs

    parts2, gs2 = backward(w2, mine2, s2)
    got2, row2 = scatter(parts2)
    w1 = load(1, row2)
    joined = gather_first(first_rows, row2)
    v = along_second([joined] * 4)
    (back1,) = call(
        grad_kernel,
        [(block, BF16)],
        [VM] * 5,
        (got2, gain[2], mine2, s2, x2),
        deps=(w1, joined),
    )
    back1 = move(back1, other_zh)
    (mine1,) = call(dots_kernel, [((R, H), BF16)], [VM] * 2, (back1, p1))
    parts1, gs1 = backward(w1, mine1, s1)

    f3_all, keep_t, send_t = call(
        order_kernel,
        [((N, M, H), BF16), ((N, H, 2 * M), BF16), ((N, H, 2 * M), BF16)],
        [VM] * 16,
        (*v, *g0, *g1, *g2),
        limit=14,
        deps=(gs1,),
    )
    recv_t = move(send_t, other_core)
    keep, send = call(last_forward_kernel, [(block, F32)] * 2, [VM] * 2, (f3_all, load(3, gs1)), **MATMUL)
    got1, row1 = scatter(parts1, send)
    recv = move(send, other_core)
    (x4,) = call(last_combine_kernel, [(block, BF16)], [VM] * 4, (keep, recv, x3, s3))
    is_first = e == 0
    shown = jnp.where(is_first, x4, x3)
    got = move(jnp.where(is_first, x3, x4), other_core)
    last = jnp.where(c == 0, jnp.concatenate([shown, got], 1), jnp.concatenate([got, shown], 1))

    gs3 = (cot.astype(F32) * s3[0][:, None]).astype(BF16)
    high = jnp.where(c == 0, gs2, gs3)
    local = jnp.where(zh == 0, gs1, high)
    far = move(jnp.where(zh == 0, high, gs1), other_zh)
    factor = jnp.repeat(jnp.exp2(-exponents[0].astype(F32)), H, axis=1).reshape(N, 2, 1, 2 * H)
    (mine0,) = call(
        grad_kernel,
        [(block, BF16)],
        [VM] * 6,
        (got1, gain[1], mine1, s1, x1, s0),
        deps=(factor, local),
    )
    far0 = move_some(mine0, other_zh, [(1, 0)])
    far1 = move_some(mine0, other_both, [(1, 1)])
    core = move_some(mine0, other_core, [(0, 1)])
    (total,) = call(
        weight_grad_kernel,
        [((N, 2, H, 2 * H), BF16)],
        [VM] * 9,
        (keep_t, recv_t, local, far, mine0, core, far0, far1, factor),
        scratch=[pltpu.VMEM((N, 2, H, 2 * H), BF16), pltpu.SemaphoreType.DMA((8,))],
        out_specs=[HBM],
        flops=2 * 256 * 256 * D,
        bytes_accessed=8 << 20,
        limit=11,
    )
    return (total.reshape(1, D, 2 * H), last[None])


def solution(mesh):
    return jax.shard_map(
        on_device,
        mesh=mesh,
        in_specs=(
            P(None, None, "dp"),
            P(None, None, "dp"),
            P(None, "pipe", None, "dp"),
            P(None, "pipe", "dp"),
            P("pipe", None, "dp"),
        ),
        out_specs=(P("pipe", None, "dp"), P("pipe", None, "dp")),
        check_vma=False,
    )
```

```python
import functools

import jax
import jax.numpy as jnp
from jax import lax
from jax.experimental import pallas as pl
from jax.experimental.pallas import tpu as pltpu
from jax.sharding import PartitionSpec as P

D = 8192
EPS = 1e-05
M = 128
H = 128
N = 32
R = M + 16
F32 = jnp.float32
BF16 = jnp.bfloat16
BOTH = ("pipe", "dp")
VM = pl.BlockSpec(memory_space=pltpu.VMEM)
HBM = pl.BlockSpec(memory_space=pltpu.HBM)
MIB = 1 << 20


def pairs(fn):
    out = []
    for i in range(128):
        p, d = divmod(i, 32)
        zh, c = divmod(p, 2)
        zl, r = divmod(d, 16)
        y, x = divmod(r, 4)
        zh2, c2, zl2, y2, x2 = fn(zh, c, zl, y, x)
        out.append((i, (zh2 * 2 + c2) * 32 + zl2 * 16 + (y2 % 4) * 4 + x2 % 4))
    return out


def move(value, fn):
    return lax.ppermute(value, BOTH, pairs(fn))


def move_some(value, fn, keep):
    return lax.ppermute(value, BOTH, [(i, j) for i, j in pairs(fn) if (i // 64, i // 32 % 2) in keep])


def other_core(zh, c, zl, y, x):
    return (zh, 1 - c, zl, y, x)


def other_zh(zh, c, zl, y, x):
    return (1 - zh, c, zl, y, x)


def other_zl(zh, c, zl, y, x):
    return (zh, c, 1 - zl, y, x)


def first_axis(k):
    return lambda zh, c, zl, y, x: (zh, c, zl, y + (k if c else 0), x + (0 if c else k))


def second_axis(k):
    return lambda zh, c, zl, y, x: (zh, c, zl, y + (0 if c else k), x + (k if c else 0))


def along_y(k):
    return lambda zh, c, zl, y, x: (zh, c, zl, y + k, x)


SHIFTS = (0, 1, 3, 2)


def place():
    p = lax.axis_index("pipe")
    return p // 2, p % 2


def block_index(sign, other=False):
    _, c = place()
    c = 1 - c if other else c
    dp = lax.axis_index("dp")
    y, x = (dp // 4) % 4, dp % 4
    b = jnp.where(c == 0, y, x)
    sa = jnp.where(c == 0, 1, 4)
    sb = jnp.where(c == 0, 4, 1)

    def index(ib, i):
        return lax.rem(b + 4 + sign * SHIFTS[ib], 4) * sb + (i % 4) * sa + (i // 4) * 16

    return index


def step_index():
    _, c = place()
    dp = lax.axis_index("dp")
    zl, y, x = dp // 16, (dp // 4) % 4, dp % 4
    a = jnp.where(c == 0, x, y)
    b = jnp.where(c == 0, y, x)
    sa = jnp.where(c == 0, 1, 4)
    sb = jnp.where(c == 0, 4, 1)

    def index(ib, ia, iz):
        jb = lax.rem(b + 4 - SHIFTS[ib], 4) * sb
        ja = lax.rem(a + 4 - SHIFTS[ia], 4) * sa
        return jb + ja + (zl if iz == 0 else 1 - zl) * 16

    return index


def to_rows(value):
    return jnp.sum(jnp.transpose(value), axis=0, keepdims=True)


def to_cols(row):
    return jnp.transpose(jnp.broadcast_to(row, (M, H)))


def extra_rows(row):
    high = row.astype(BF16)
    low = (row - high.astype(F32)).astype(BF16)
    i = lax.broadcasted_iota(jnp.int32, (16, M), 0)
    value = jnp.where(i == 0, high.astype(F32), jnp.where(i == 1, low.astype(F32), 0.0))
    return value.astype(BF16)


def read_extra(block):
    return jnp.sum(block.astype(F32), axis=0, keepdims=True)


def split_kernel(w_ref, own_ref, send_ref, sem):
    _, c = place()
    copies = [pltpu.make_async_copy(w_ref.at[b, :, 1 - c], send_ref.at[b], sem.at[b]) for b in range(2)]
    copies += [pltpu.make_async_copy(w_ref.at[b, :, c], own_ref.at[b], sem.at[2 + b]) for b in range(2)]
    for copy in copies:
        copy.start()
    for copy in copies:
        copy.wait()


def pick_kernel(own_ref, other_ref, out_ref, sem):
    zh, c = place()

    def run(own_ticks, other_ticks):
        copies = []
        for i in range(2):
            b = zh if i == 0 else 1 - zh
            copies.append(pltpu.make_async_copy(own_ref.at[b], out_ref.at[own_ticks[i]], sem.at[i]))
            copies.append(pltpu.make_async_copy(other_ref.at[b], out_ref.at[other_ticks[i]], sem.at[2 + i]))
        for copy in copies:
            copy.start()
        for copy in copies:
            copy.wait()

    pl.when((zh ^ c) == 0)(lambda: run((0, 3), (1, 2)))
    pl.when((zh ^ c) == 1)(lambda: run((1, 2), (0, 3)))


def load_kernel(tick, w_ref, out_ref, sem):
    parts = [pl.ds(N // 8 * i, N // 8) for i in range(8)]
    copies = [pltpu.make_async_copy(w_ref.at[tick, q], out_ref.at[q], sem.at[i]) for i, q in enumerate(parts)]
    for copy in copies:
        copy.start()
    for copy in copies:
        copy.wait()


def payload_kernel(x_ref, gain_ref, out_ref, ft_ref):
    x = x_ref[...].astype(F32)
    f = (x * gain_ref[...].astype(F32)).astype(BF16)
    ft_ref[...] = jnp.transpose(f)
    extra = extra_rows(to_rows(x * x))
    for j in range(out_ref.shape[0]):
        out_ref[j, 0:M, :] = f
        out_ref[j, M:R, :] = extra


def forward_kernel(v0, v1, v2, v3, w_ref, keep_ref, send_ref):
    _, c = place()
    index = block_index(-1)
    sums = jnp.zeros((16, M), F32)
    total = jnp.zeros((M, 2 * H), F32)
    for ref in (v0, v1, v2, v3):
        sums = sums + jnp.sum(ref[:, M:R, :].astype(F32), axis=0)
    for ib, ref in enumerate((v0, v1, v2, v3)):
        f = jnp.concatenate([ref[i, 0:M, :] for i in range(8)], axis=1)
        w = jnp.concatenate([w_ref[index(ib, i)] for i in range(8)], axis=0)
        total = total + jnp.dot(f, w, preferred_element_type=F32)
    sums = jnp.broadcast_to(jnp.sum(sums, axis=0, keepdims=True), (8, M))
    first = c == 0
    keep_ref[0:M, :] = jnp.where(first, total[:, :H], total[:, H:])
    send_ref[0:M, :] = jnp.where(first, total[:, H:], total[:, :H])
    keep_ref[M : M + 8, :] = sums
    send_ref[M : M + 8, :] = sums


def last_forward_kernel(v0, v1, v2, v3, w_ref, keep_ref, send_ref):
    _, c = place()
    index = step_index()
    total = jnp.zeros((M, 2 * H), F32)
    for ib, ref in enumerate((v0, v1, v2, v3)):
        f = jnp.concatenate([ref[at, 0] for at in range(8)], axis=1)
        w = jnp.concatenate([w_ref[index(ib, at // 2, at % 2)] for at in range(8)], axis=0)
        total = total + jnp.dot(f, w, preferred_element_type=F32)
    first = c == 0
    keep_ref[...] = jnp.where(first, total[:, :H], total[:, H:])
    send_ref[...] = jnp.where(first, total[:, H:], total[:, :H])


def combine_kernel(keep_ref, recv_ref, x_ref, gain_ref, next_ref, p_ref, s_ref, out_ref=None, ft_ref=None):
    squares = keep_ref[M : M + 8, :] + recv_ref[M : M + 8, :]
    scale = lax.rsqrt(squares / D + EPS)
    s_ref[...] = scale
    p = keep_ref[0:M, :] + recv_ref[0:M, :]
    p_ref[...] = p
    new = (x_ref[...].astype(F32) + to_cols(scale[0:1]) * p).astype(BF16)
    next_ref[...] = new
    if out_ref is not None:
        x = new.astype(F32)
        f = (x * gain_ref[...].astype(F32)).astype(BF16)
        ft_ref[...] = jnp.transpose(f)
        extra = extra_rows(to_rows(x * x))
        for j in range(out_ref.shape[0]):
            out_ref[j, 0:M, :] = f
            out_ref[j, M:R, :] = extra


def third_combine_kernel(keep_ref, recv_ref, x_ref, gain_ref, gn_ref, next_ref, p_ref, s_ref, f_ref, ft_ref, sums_ref):
    squares = keep_ref[M : M + 8, :] + recv_ref[M : M + 8, :]
    scale = lax.rsqrt(squares / D + EPS)
    s_ref[...] = scale
    p = keep_ref[0:M, :] + recv_ref[0:M, :]
    p_ref[...] = p
    new = (x_ref[...].astype(F32) + to_cols(scale[0:1]) * p).astype(BF16)
    next_ref[...] = new
    x = new.astype(F32)
    f = (x * gain_ref[...].astype(F32)).astype(BF16)
    f_ref[...] = f
    ft_ref[...] = jnp.transpose(f)
    i = lax.broadcasted_iota(jnp.int32, (8, M), 0)
    sums = jnp.where(i == 0, to_rows(x * x), jnp.where(i == 1, to_rows(x * gn_ref[...]), 0.0))
    for j in range(16):
        sums_ref[j] = sums


def last_combine_kernel(keep_ref, recv_ref, x_ref, s_ref, shown_ref, send_ref):
    zh, c = place()
    p = keep_ref[...] + recv_ref[...]
    x = x_ref[...]
    new = (x.astype(F32) + to_cols(s_ref[0:1, :]) * p).astype(BF16)
    shown_ref[...] = jnp.where((zh ^ c) == 0, new, x)
    send_ref[...] = jnp.where((zh ^ c) == 0, x, new)


def turned(left, right):
    return jnp.concatenate([jnp.transpose(left), jnp.transpose(right)], axis=0)


def backward_kernel(mine_ref, theirs_ref, s_ref, w_ref, *refs):
    extra_refs = refs[:-5] if len(refs) == 5 else refs[:2]
    o0, o1, o2, o3 = refs[len(extra_refs) : len(extra_refs) + 4]
    zh, c = place()
    first = c == 0
    a = mine_ref[0:M, :]
    b = theirs_ref[0:M, :]
    left = jnp.where(first, a, b)
    right = jnp.where(first, b, a)
    scale = to_cols(s_ref[0:1, :])
    scaled = jnp.concatenate([left.astype(F32) * scale, right.astype(F32) * scale], axis=1).astype(BF16)
    if extra_refs:
        high = jnp.where(first, extra_refs[0][...], extra_refs[1][...])
        refs[-2][...] = jnp.where(zh == 0, scaled, high)
        refs[-1][...] = jnp.where(zh == 0, high, scaled)
    else:
        refs[-1][...] = scaled
    extra = extra_rows(read_extra(mine_ref[M:R, :]) + read_extra(theirs_ref[M:R, :]))
    gt = turned(left, right)
    index = block_index(1)
    for ib, ref in enumerate((o0, o1, o2, o3)):
        w = jnp.concatenate([w_ref[index(ib, i)] for i in range(8)], axis=0)
        ref[:, 0:M, :] = jnp.dot(w, gt, preferred_element_type=F32).astype(BF16).reshape(8, H, M)
        for i in range(8):
            ref[i, M:R, :] = extra


def first_backward_kernel(g_ref, w_ref, o0, o1, o2, o3):
    gt = turned(g_ref[:, :H], g_ref[:, H:])
    index = block_index(1)
    for ib, ref in enumerate((o0, o1, o2, o3)):
        w = jnp.concatenate([w_ref[index(ib, i)] for i in range(8)], axis=0)
        ref[...] = jnp.dot(w, gt, preferred_element_type=F32).astype(BF16).reshape(8, H, M)


def sum_kernel(r0, r1, r2, r3, out):
    total = r0[...].astype(F32) + r1[...].astype(F32) + r2[...].astype(F32) + r3[...].astype(F32)
    out[:, 0:M, :] = total[:, 0:M, :].astype(BF16)
    if total.shape[1] == R:
        for i in range(8):
            out[i, M:R, :] = extra_rows(jnp.sum(total[i, M:R, :], axis=0, keepdims=True))


def last_sum_kernel(got_ref, gain_ref, gn_ref):
    total = jnp.sum(got_ref[...].astype(F32), axis=0)
    gn_ref[...] = jnp.transpose(total) * gain_ref[...].astype(F32)


def choose_kernel(a_ref, b_ref, out):
    zh, _ = place()
    out[...] = jnp.where(zh == 0, a_ref[...], b_ref[...])


def join_kernel(r0, r1, r2, r3, out):
    n = r0.shape[0]
    for i, ref in enumerate((r0, r1, r2, r3)):
        out[i * n : (i + 1) * n] = ref[...]


def turned(left, right):
    return jnp.concatenate([jnp.transpose(left), jnp.transpose(right)], axis=0)


def add_kernel(r, out):
    out[...] = jnp.sum(r[...], axis=0)


def last_grad_kernel(s0, s1, s2, s3, cot_ref, gn_ref, x_ref, p_ref, out_ref, s_ref, gs_ref):
    total = s0[...] + s1[...] + s2[...] + s3[...]
    scale = lax.rsqrt(total[0:1, :] / D + EPS)
    s_ref[...] = jnp.broadcast_to(scale, (8, M))
    mix = scale * scale * scale * total[1:2, :] / D
    _, c = place()
    column = to_cols(scale)
    left, right = cot_ref[:, :H].astype(F32), cot_ref[:, H:].astype(F32)
    gs_ref[...] = jnp.concatenate([left * column, right * column], axis=1).astype(BF16)
    g = jnp.where(c == 0, left, right) + column * gn_ref[...] - to_cols(mix) * x_ref[...].astype(F32)
    g = g.astype(BF16)
    out_ref[0:M, :] = g
    out_ref[M:R, :] = extra_rows(to_rows(g.astype(F32) * p_ref[...]))


def grad_kernel(got_ref, gain_ref, g_ref, s_ref, x_ref, *rest):
    out_ref = rest[-1]
    total = jnp.sum(got_ref[:, 0:M, :].astype(F32), axis=0)
    dots = jnp.sum(jnp.sum(got_ref[:, M:R, :].astype(F32), axis=0), axis=0, keepdims=True)
    gn = jnp.transpose(total) * gain_ref[...].astype(F32)
    scale = s_ref[0:1, :]
    mix = scale * scale * scale * dots / D
    g = g_ref[0:M, :].astype(F32) + to_cols(scale) * gn - to_cols(mix) * x_ref[...].astype(F32)
    if len(rest) == 2:
        g = g.astype(BF16).astype(F32) * to_cols(rest[0][0:1, :])
    out_ref[...] = g.astype(BF16)


def dots_kernel(g_ref, p_ref, out_ref):
    g = g_ref[...]
    out_ref[0:M, :] = g
    out_ref[M:R, :] = extra_rows(to_rows(g.astype(F32) * p_ref[...]))


def order_kernel(*refs):
    v, g0, g1, g2 = refs[0:4], refs[4:8], refs[8:12], refs[12:16]
    keep, send = refs[16:20], refs[20:24]
    zh, c = place()
    dp = lax.axis_index("dp")
    zl, y, x = dp // 16, (dp // 4) % 4, dp % 4
    a = jnp.where(c == 0, x, y)

    def at(ia, iz):
        return (zl if iz == 0 else 1 - zl) * 4 + lax.rem(a + 4 - SHIFTS[ia], 4)

    def fill(first, second, q0, q1):
        for ib in range(4):
            for i in range(8):
                q0[ib][i, :, :M] = jnp.transpose(first[ib][i, 0:M, :])
                if second is not None:
                    q1[ib][i, :, :M] = jnp.transpose(second[ib][i, 0:M, :])
            for ia in range(4):
                for iz in range(2):
                    i = at(ia, iz)
                    q0[ib][i, :, M:] = v[ib][ia * 2 + iz, 1]
                    q1[ib][i, :, M:] = v[ib][ia * 2 + iz, 2]
                    if second is None:
                        q1[ib][i, :, :M] = jnp.transpose(v[ib][ia * 2 + iz, 0])

    for half in range(2):
        for core in range(2):
            q0, q1 = (keep, send) if core == 0 else (send, keep)
            first, second = (g0, g1) if half == 0 else (g2, None)
            pl.when(jnp.logical_and(zh == half, c == core))(functools.partial(fill, first, second, q0, q1))


def weight_grad_kernel(*refs):
    keep, recv = refs[0:4], refs[4:8]
    local_ref, far_ref, late_ref, far_late_ref, factor_ref, out_ref, buf, sem = refs[8:]
    zh, c = place()
    late = (zh + c) == 0
    local = jnp.where(late, late_ref[...], local_ref[...])
    far = jnp.where(late, far_late_ref[...], far_ref[...])
    g = jnp.concatenate([local, far], axis=0)
    for features, which, index in ((keep, c, block_index(-1)), (recv, 1 - c, block_index(-1, True))):
        for ib, ref in enumerate(features):
            value = jnp.dot(ref[...].reshape(8 * H, 2 * M), g, preferred_element_type=F32).reshape(8, H, 2 * H)
            for i in range(8):
                j = index(ib, i)
                buf[j, which] = (value[i] * factor_ref[j, which]).astype(BF16)
                pltpu.make_async_copy(buf.at[j, which], out_ref.at[j, which], sem).start()
    pltpu.make_async_copy(buf, out_ref, sem).wait()


def call(kernel, out, specs, args, scratch=(), flops=0, bytes_accessed=0, limit=4, out_specs=None, deps=()):
    count = len(args)

    def body(*refs):
        kernel(*refs[:count], *refs[count + len(deps) :])

    return pl.pallas_call(
        body,
        out_shape=[jax.ShapeDtypeStruct(s, d) for s, d in out],
        in_specs=list(specs) + [pl.BlockSpec(memory_space=pl.ANY)] * len(deps),
        out_specs=out_specs or [VM] * len(out),
        scratch_shapes=list(scratch),
        compiler_params=pltpu.CompilerParams(vmem_limit_bytes=limit * MIB),
        cost_estimate=pl.CostEstimate(flops=flops, bytes_accessed=bytes_accessed, transcendentals=0),
    )(*args, *deps)


MATMUL = dict(
    flops=2 * M * N * H * 2 * H,
    bytes_accessed=4 << 20,
    limit=6,
)


def plane_groups():
    groups = {}
    for i in range(128):
        p, d = divmod(i, 32)
        c = p % 2
        y, x = (d // 4) % 4, d % 4
        groups.setdefault((p, y if c == 0 else x), []).append((d // 16, x if c == 0 else y, i))
    return [[i for _, _, i in sorted(g)] for g in groups.values()]


PLANES = plane_groups()


def core_groups():
    groups = {}
    for i in range(128):
        p, d = divmod(i, 32)
        groups.setdefault((p // 2, (d // 4) % 4), []).append(i)
    return list(groups.values())


CORES = core_groups()


def exchange(value):
    return lax.all_to_all(value, BOTH, 0, 0, axis_index_groups=PLANES)


def along_second(parts):
    return [parts[0]] + [move(parts[i], second_axis(SHIFTS[i])) for i in (1, 2, 3)]


def gather(payload):
    row = exchange(payload)
    return along_second([row] * 4)


def scatter(parts, *deps):
    shape = parts[0].shape
    (total,) = call(sum_kernel, [(shape, BF16)], [VM] * 4, along_second(parts), deps=deps)
    return exchange(total), total


def gather_z(value):
    return jnp.stack([value, move(value, other_zl)])


def gather_first(both, dep):
    rows = [both] + [move(both, first_axis(k)) for k in SHIFTS[1:]]
    return call(join_kernel, [((8,) + both.shape[1:], BF16)], [VM] * 4, rows, deps=(dep,))[0]


def on_device(batches, cotangents, weights, gains, exponents):
    zh, c = place()
    e = zh ^ c
    w5 = weights.reshape(2, N, 2, H, 2 * H)

    def half(value, which):
        return lax.dynamic_slice_in_dim(value, which * H, H, axis=value.ndim - 1)

    own_gain = half(gains[:, 0], c)
    got_gain = move(half(gains[:, 0], 1 - c), other_core)
    gain = []
    for tick in range(4):
        copy_index = zh if tick < 2 else 1 - zh
        own = (e == 0) if tick in (0, 3) else (e == 1)
        both = jnp.where(own, own_gain, got_gain)
        gain.append(lax.dynamic_slice_in_dim(both, copy_index, 1, axis=0))

    x0 = half(lax.dynamic_index_in_dim(batches, zh, axis=0, keepdims=False), c)
    block = (M, H)
    wide = ((8, R, H), BF16)
    out0, ft0 = call(payload_kernel, [wide, (block, BF16)], [VM] * 2, (x0, gain[0]))
    g0 = gather(out0)

    started = move(ft0, other_core)
    own_w, send_w = call(
        split_kernel,
        [((2, N, H, 2 * H), BF16)] * 2,
        [VM],
        (w5,),
        scratch=[pltpu.SemaphoreType.DMA((4,))],
        out_specs=[HBM] * 2,
        limit=10,
        deps=(started,),
    )
    (all_w,) = call(
        pick_kernel,
        [((24, N, H, 2 * H), BF16)],
        [VM] * 2,
        (own_w, move(send_w, other_core)),
        scratch=[pltpu.SemaphoreType.DMA((4,))],
        out_specs=[HBM],
        limit=10,
    )

    def load(tick, *deps):
        return call(
            functools.partial(load_kernel, tick),
            [((N, H, 2 * H), BF16)],
            [HBM],
            (all_w,),
            scratch=[pltpu.SemaphoreType.DMA((8,))],
            deps=deps,
        )[0]

    cot = lax.dynamic_index_in_dim(cotangents, 1 - zh, axis=0, keepdims=False)
    first_parts = call(first_backward_kernel, [((8, H, M), BF16)] * 4, [VM] * 2, (cot, load(3)), **MATMUL)
    parts = along_second(first_parts)

    def forward(weight, gathered, deps):
        keep, send = call(
            forward_kernel, [((M + 8, H), F32)] * 2, [VM] * 5, (*gathered, weight), deps=deps, **MATMUL
        )
        return keep, move(send, other_core)

    outs = [(block, BF16), (block, F32), ((8, M), F32)]
    keep, recv = forward(load(0), g0, first_parts)
    x1, _, s0, out1, ft1 = call(
        combine_kernel, outs + [wide, (block, BF16)], [VM] * 4, (keep, recv, x0, gain[1])
    )
    g1 = gather(out1)
    (row3,) = call(sum_kernel, [((8, H, M), BF16)], [VM] * 4, parts)
    (gn3,) = call(last_sum_kernel, [(block, F32)], [VM] * 2, (exchange(row3), gain[3]))
    keep, recv = forward(load(1, out1), g1, ())
    x2, p1, s1 = call(combine_kernel, outs, [VM] * 4, (keep, recv, x1, gain[1]), deps=(gn3,))
    x2 = move(x2, other_zh)
    out2, ft2 = call(payload_kernel, [wide, (block, BF16)], [VM] * 2, (x2, gain[2]))
    g2 = gather(out2)
    mirror0 = move(jnp.where(zh == 1, ft0, ft2), other_zh)
    keep, recv = forward(load(2, out2), g2, (mirror0,))
    x3, p2, s2, f3, ft3, spread = call(
        third_combine_kernel,
        outs + [(block, BF16), (block, BF16), ((16, 8, M), F32)],
        [VM] * 5,
        (keep, recv, x2, gain[3], gn3),
    )
    (sums,) = call(add_kernel, [((8, M), F32)], [VM], (lax.all_to_all(spread, BOTH, 0, 0, axis_index_groups=CORES),))
    (send3,) = call(choose_kernel, [(block, BF16)], [VM] * 2, (ft3, ft1), deps=(sums,))
    mirror1 = move(send3, other_zh)
    first_rows = gather_z(jnp.stack([f3, mirror0, mirror1]))
    w2 = load(2, x3)
    sums = [sums] + [move(sums, along_y(k)) for k in SHIFTS[1:]]

    mine2, s3, gs3 = call(
        last_grad_kernel,
        [((R, H), BF16), ((8, M), F32), ((M, 2 * H), BF16)],
        [VM] * 8,
        (*sums, cot, gn3, x3, p2),
        deps=(w2, mirror1),
    )

    def backward(weight, mine, s, *deps, extra=()):
        theirs = move(mine, other_core)
        outs = [wide] * 4 + [((M, 2 * H), BF16)] * (2 if extra else 1)
        args = (mine, theirs, s, weight, *extra)
        *parts, last = call(backward_kernel, outs, [VM] * len(args), args, deps=deps, **MATMUL)
        return (parts[:4], *parts[4:], last)

    parts2, gs2 = backward(w2, mine2, s2)
    factor = jnp.repeat(jnp.exp2(-exponents[0].astype(F32)), H, axis=1).reshape(N, 2, 1, 2 * H)
    got2, row2 = scatter(parts2)
    w1 = load(1, row2)
    joined = gather_first(first_rows, row2)
    v = along_second([joined] * 4)
    (back1,) = call(
        grad_kernel,
        [(block, BF16)],
        [VM] * 5,
        (got2, gain[2], mine2, s2, x2),
        deps=(w1,),
    )
    moved1 = move(back1, other_zh)
    (mine1,) = call(dots_kernel, [((R, H), BF16)], [VM] * 2, (moved1, p1), deps=(factor,))
    parts1, local, far = backward(w1, mine1, s1, extra=(gs2, gs3))
    gs1 = local
    keep, send = call(last_forward_kernel, [(block, F32)] * 2, [VM] * 5, (*v, load(3, gs1)), deps=(gs1,), **MATMUL)
    got1, _ = scatter(parts1, keep)
    far = move(far, other_zh)
    turned_features = call(
        order_kernel, [((8, H, 2 * M), BF16)] * 8, [VM] * 16, (*v, *g0, *g1, *g2), limit=14, deps=(gs1,)
    )
    kept, received = turned_features[:4], [move(t, other_core) for t in turned_features[4:]]

    recv = move(send, other_core)
    shown, got = call(last_combine_kernel, [(block, BF16)] * 2, [VM] * 4, (keep, recv, x3, s3))
    got = move(got, other_core)
    last = jnp.where(c == 0, jnp.concatenate([shown, got], 1), jnp.concatenate([got, shown], 1))

    (mine0,) = call(
        grad_kernel,
        [(block, BF16)],
        [VM] * 6,
        (got1, gain[1], mine1, s1, x1, s0),
    )
    late = jnp.concatenate([mine0, move_some(mine0, other_core, [(0, 1), (1, 1)])], axis=1)
    far_late = move_some(late, other_zh, [(1, 0)])
    (total,) = call(
        weight_grad_kernel,
        [((N, 2, H, 2 * H), BF16)],
        [VM] * 13,
        (*kept, *received, local, far, late, far_late, factor),
        scratch=[pltpu.VMEM((N, 2, H, 2 * H), BF16), pltpu.SemaphoreType.DMA],
        out_specs=[HBM],
        flops=2 * 256 * 256 * D,
        bytes_accessed=8 << 20,
        limit=11,
    )
    return (total.reshape(1, D, 2 * H), last[None])


def solution(mesh):
    return jax.shard_map(
        on_device,
        mesh=mesh,
        in_specs=(
            P(None, None, "dp"),
            P(None, None, "dp"),
            P(None, "pipe", None, "dp"),
            P(None, "pipe", "dp"),
            P("pipe", None, "dp"),
        ),
        out_specs=(P("pipe", None, "dp"), P("pipe", None, "dp")),
        check_vma=False,
    )
```

```python
import functools

import jax
import jax.numpy as jnp
from jax import lax
from jax.experimental import pallas as pl
from jax.experimental.pallas import tpu as pltpu
from jax.sharding import PartitionSpec as P

D = 8192
EPS = 1e-05
M = 128
H = 128
N = 32
R = M + 16
F32 = jnp.float32
BF16 = jnp.bfloat16
BOTH = ("pipe", "dp")
VM = pl.BlockSpec(memory_space=pltpu.VMEM)
HBM = pl.BlockSpec(memory_space=pltpu.HBM)
MIB = 1 << 20


def pairs(fn):
    out = []
    for i in range(128):
        p, d = divmod(i, 32)
        zh, c = divmod(p, 2)
        zl, r = divmod(d, 16)
        y, x = divmod(r, 4)
        zh2, c2, zl2, y2, x2 = fn(zh, c, zl, y, x)
        out.append((i, (zh2 * 2 + c2) * 32 + zl2 * 16 + (y2 % 4) * 4 + x2 % 4))
    return out


def move(value, fn):
    return lax.ppermute(value, BOTH, pairs(fn))


def move_some(value, fn, keep):
    return lax.ppermute(value, BOTH, [(i, j) for i, j in pairs(fn) if (i // 64, i // 32 % 2) in keep])


def other_core(zh, c, zl, y, x):
    return (zh, 1 - c, zl, y, x)


def other_zh(zh, c, zl, y, x):
    return (1 - zh, c, zl, y, x)


def other_zl(zh, c, zl, y, x):
    return (zh, c, 1 - zl, y, x)


def first_axis(k):
    return lambda zh, c, zl, y, x: (zh, c, zl, y + (k if c else 0), x + (0 if c else k))


def second_axis(k):
    return lambda zh, c, zl, y, x: (zh, c, zl, y + (0 if c else k), x + (k if c else 0))


def along_y(k):
    return lambda zh, c, zl, y, x: (zh, c, zl, y + k, x)


SHIFTS = (0, 1, 3, 2)


def place():
    p = lax.axis_index("pipe")
    return p // 2, p % 2


def block_index(sign, other=False):
    _, c = place()
    c = 1 - c if other else c
    dp = lax.axis_index("dp")
    y, x = (dp // 4) % 4, dp % 4
    b = jnp.where(c == 0, y, x)
    sa = jnp.where(c == 0, 1, 4)
    sb = jnp.where(c == 0, 4, 1)

    def index(ib, i):
        return lax.rem(b + 4 + sign * SHIFTS[ib], 4) * sb + (i % 4) * sa + (i // 4) * 16

    return index


def step_index():
    _, c = place()
    dp = lax.axis_index("dp")
    zl, y, x = dp // 16, (dp // 4) % 4, dp % 4
    a = jnp.where(c == 0, x, y)
    b = jnp.where(c == 0, y, x)
    sa = jnp.where(c == 0, 1, 4)
    sb = jnp.where(c == 0, 4, 1)

    def index(ib, ia, iz):
        jb = lax.rem(b + 4 - SHIFTS[ib], 4) * sb
        ja = lax.rem(a + 4 - SHIFTS[ia], 4) * sa
        return jb + ja + (zl if iz == 0 else 1 - zl) * 16

    return index


def to_rows(value):
    return jnp.sum(jnp.transpose(value), axis=0, keepdims=True)


def to_cols(row):
    return jnp.transpose(jnp.broadcast_to(row, (M, H)))


def extra_rows(row):
    high = row.astype(BF16)
    low = (row - high.astype(F32)).astype(BF16)
    i = lax.broadcasted_iota(jnp.int32, (16, M), 0)
    value = jnp.where(i == 0, high.astype(F32), jnp.where(i == 1, low.astype(F32), 0.0))
    return value.astype(BF16)


def read_extra(block):
    return jnp.sum(block.astype(F32), axis=0, keepdims=True)


def split_kernel(w_ref, own_ref, send_ref, sem):
    _, c = place()
    copies = [pltpu.make_async_copy(w_ref.at[b, :, 1 - c], send_ref.at[b], sem.at[b]) for b in range(2)]
    copies += [pltpu.make_async_copy(w_ref.at[b, :, c], own_ref.at[b], sem.at[2 + b]) for b in range(2)]
    for copy in copies:
        copy.start()
    for copy in copies:
        copy.wait()


def pick_kernel(own_ref, other_ref, out_ref, sem):
    zh, c = place()

    def run(own_ticks, other_ticks):
        copies = []
        for i in range(2):
            b = zh if i == 0 else 1 - zh
            copies.append(pltpu.make_async_copy(own_ref.at[b], out_ref.at[own_ticks[i]], sem.at[i]))
            copies.append(pltpu.make_async_copy(other_ref.at[b], out_ref.at[other_ticks[i]], sem.at[2 + i]))
        for copy in copies:
            copy.start()
        for copy in copies:
            copy.wait()

    pl.when((zh ^ c) == 0)(lambda: run((0, 3), (1, 2)))
    pl.when((zh ^ c) == 1)(lambda: run((1, 2), (0, 3)))


def load_kernel(tick, w_ref, out_ref, sem):
    parts = [pl.ds(N // 8 * i, N // 8) for i in range(8)]
    copies = [pltpu.make_async_copy(w_ref.at[tick, q], out_ref.at[q], sem.at[i]) for i, q in enumerate(parts)]
    for copy in copies:
        copy.start()
    for copy in copies:
        copy.wait()


def payload_kernel(x_ref, gain_ref, out_ref, ft_ref):
    x = x_ref[...].astype(F32)
    f = (x * gain_ref[...].astype(F32)).astype(BF16)
    ft_ref[...] = jnp.transpose(f)
    extra = extra_rows(to_rows(x * x))
    for j in range(out_ref.shape[0]):
        out_ref[j, 0:M, :] = f
        out_ref[j, M:R, :] = extra


def forward_kernel(v0, v1, v2, v3, w_ref, keep_ref, send_ref):
    _, c = place()
    index = block_index(-1)
    sums = jnp.zeros((16, M), F32)
    total = jnp.zeros((M, 2 * H), F32)
    for ref in (v0, v1, v2, v3):
        sums = sums + jnp.sum(ref[:, M:R, :].astype(F32), axis=0)
    for ib, ref in enumerate((v0, v1, v2, v3)):
        f = jnp.concatenate([ref[i, 0:M, :] for i in range(8)], axis=1)
        w = jnp.concatenate([w_ref[index(ib, i)] for i in range(8)], axis=0)
        total = total + jnp.dot(f, w, preferred_element_type=F32)
    sums = jnp.broadcast_to(jnp.sum(sums, axis=0, keepdims=True), (8, M))
    first = c == 0
    keep_ref[0:M, :] = jnp.where(first, total[:, :H], total[:, H:])
    send_ref[0:M, :] = jnp.where(first, total[:, H:], total[:, :H])
    keep_ref[M : M + 8, :] = sums
    send_ref[M : M + 8, :] = sums


def last_forward_kernel(v0, v1, v2, v3, w_ref, keep_ref, send_ref):
    _, c = place()
    index = step_index()
    total = jnp.zeros((M, 2 * H), F32)
    for ib, ref in enumerate((v0, v1, v2, v3)):
        f = jnp.concatenate([ref[at, 0] for at in range(8)], axis=1)
        w = jnp.concatenate([w_ref[index(ib, at // 2, at % 2)] for at in range(8)], axis=0)
        total = total + jnp.dot(f, w, preferred_element_type=F32)
    first = c == 0
    keep_ref[...] = jnp.where(first, total[:, :H], total[:, H:])
    send_ref[...] = jnp.where(first, total[:, H:], total[:, :H])


def combine_kernel(keep_ref, recv_ref, x_ref, gain_ref, next_ref, p_ref, s_ref, out_ref=None, ft_ref=None):
    squares = keep_ref[M : M + 8, :] + recv_ref[M : M + 8, :]
    scale = lax.rsqrt(squares / D + EPS)
    s_ref[...] = scale
    p = keep_ref[0:M, :] + recv_ref[0:M, :]
    p_ref[...] = p
    new = (x_ref[...].astype(F32) + to_cols(scale[0:1]) * p).astype(BF16)
    next_ref[...] = new
    if out_ref is not None:
        x = new.astype(F32)
        f = (x * gain_ref[...].astype(F32)).astype(BF16)
        ft_ref[...] = jnp.transpose(f)
        extra = extra_rows(to_rows(x * x))
        for j in range(out_ref.shape[0]):
            out_ref[j, 0:M, :] = f
            out_ref[j, M:R, :] = extra


def third_combine_kernel(keep_ref, recv_ref, x_ref, gain_ref, gn_ref, next_ref, p_ref, s_ref, f_ref, ft_ref, sums_ref):
    squares = keep_ref[M : M + 8, :] + recv_ref[M : M + 8, :]
    scale = lax.rsqrt(squares / D + EPS)
    s_ref[...] = scale
    p = keep_ref[0:M, :] + recv_ref[0:M, :]
    p_ref[...] = p
    new = (x_ref[...].astype(F32) + to_cols(scale[0:1]) * p).astype(BF16)
    next_ref[...] = new
    x = new.astype(F32)
    f = (x * gain_ref[...].astype(F32)).astype(BF16)
    f_ref[...] = f
    ft_ref[...] = jnp.transpose(f)
    i = lax.broadcasted_iota(jnp.int32, (8, M), 0)
    sums = jnp.where(i == 0, to_rows(x * x), jnp.where(i == 1, to_rows(x * gn_ref[...]), 0.0))
    for j in range(16):
        sums_ref[j] = sums


def last_combine_kernel(keep_ref, recv_ref, x_ref, s_ref, shown_ref, send_ref):
    zh, c = place()
    p = keep_ref[...] + recv_ref[...]
    x = x_ref[...]
    new = (x.astype(F32) + to_cols(s_ref[0:1, :]) * p).astype(BF16)
    shown_ref[...] = jnp.where((zh ^ c) == 0, new, x)
    send_ref[...] = jnp.where((zh ^ c) == 0, x, new)


def turned(left, right):
    return jnp.concatenate([jnp.transpose(left), jnp.transpose(right)], axis=0)


def backward_kernel(mine_ref, theirs_ref, s_ref, w_ref, *refs):
    extra_refs = refs[:-5] if len(refs) == 5 else refs[:2]
    o0, o1, o2, o3 = refs[len(extra_refs) : len(extra_refs) + 4]
    zh, c = place()
    first = c == 0
    a = mine_ref[0:M, :]
    b = theirs_ref[0:M, :]
    left = jnp.where(first, a, b)
    right = jnp.where(first, b, a)
    scale = to_cols(s_ref[0:1, :])
    scaled = jnp.concatenate([left.astype(F32) * scale, right.astype(F32) * scale], axis=1).astype(BF16)
    if extra_refs:
        high = jnp.where(first, extra_refs[0][...], extra_refs[1][...])
        refs[-2][...] = jnp.where(zh == 0, scaled, high)
        refs[-1][...] = jnp.where(zh == 0, high, scaled)
    else:
        refs[-1][...] = scaled
    extra = extra_rows(read_extra(mine_ref[M:R, :]) + read_extra(theirs_ref[M:R, :]))
    gt = turned(left, right)
    index = block_index(1)
    for ib, ref in enumerate((o0, o1, o2, o3)):
        w = jnp.concatenate([w_ref[index(ib, i)] for i in range(8)], axis=0)
        ref[:, 0:M, :] = jnp.dot(w, gt, preferred_element_type=F32).astype(BF16).reshape(8, H, M)
        for i in range(8):
            ref[i, M:R, :] = extra


def first_backward_kernel(g_ref, w_ref, o0, o1, o2, o3):
    gt = turned(g_ref[:, :H], g_ref[:, H:])
    index = block_index(1)
    for ib, ref in enumerate((o0, o1, o2, o3)):
        w = jnp.concatenate([w_ref[index(ib, i)] for i in range(8)], axis=0)
        ref[...] = jnp.dot(w, gt, preferred_element_type=F32).astype(BF16).reshape(8, H, M)


def sum_kernel(r0, r1, r2, r3, out):
    total = r0[...].astype(F32) + r1[...].astype(F32) + r2[...].astype(F32) + r3[...].astype(F32)
    out[:, 0:M, :] = total[:, 0:M, :].astype(BF16)
    if total.shape[1] == R:
        for i in range(8):
            out[i, M:R, :] = extra_rows(jnp.sum(total[i, M:R, :], axis=0, keepdims=True))


def last_sum_kernel(got_ref, gain_ref, gn_ref):
    total = jnp.sum(got_ref[...].astype(F32), axis=0)
    gn_ref[...] = jnp.transpose(total) * gain_ref[...].astype(F32)


def choose_kernel(a_ref, b_ref, out):
    zh, _ = place()
    out[...] = jnp.where(zh == 0, a_ref[...], b_ref[...])


def join_kernel(r0, r1, r2, r3, out):
    n = r0.shape[0]
    for i, ref in enumerate((r0, r1, r2, r3)):
        out[i * n : (i + 1) * n] = ref[...]


def turned(left, right):
    return jnp.concatenate([jnp.transpose(left), jnp.transpose(right)], axis=0)


def add_kernel(r, out):
    out[...] = jnp.sum(r[...], axis=0)


def last_grad_kernel(s0, s1, s2, s3, cot_ref, gn_ref, x_ref, p_ref, out_ref, s_ref, gs_ref):
    total = s0[...] + s1[...] + s2[...] + s3[...]
    scale = lax.rsqrt(total[0:1, :] / D + EPS)
    s_ref[...] = jnp.broadcast_to(scale, (8, M))
    mix = scale * scale * scale * total[1:2, :] / D
    _, c = place()
    column = to_cols(scale)
    left, right = cot_ref[:, :H].astype(F32), cot_ref[:, H:].astype(F32)
    gs_ref[...] = jnp.concatenate([left * column, right * column], axis=1).astype(BF16)
    g = jnp.where(c == 0, left, right) + column * gn_ref[...] - to_cols(mix) * x_ref[...].astype(F32)
    g = g.astype(BF16)
    out_ref[0:M, :] = g
    out_ref[M:R, :] = extra_rows(to_rows(g.astype(F32) * p_ref[...]))


def grad_kernel(got_ref, gain_ref, g_ref, s_ref, x_ref, *rest):
    out_ref = rest[-1]
    total = jnp.sum(got_ref[:, 0:M, :].astype(F32), axis=0)
    dots = jnp.sum(jnp.sum(got_ref[:, M:R, :].astype(F32), axis=0), axis=0, keepdims=True)
    gn = jnp.transpose(total) * gain_ref[...].astype(F32)
    scale = s_ref[0:1, :]
    mix = scale * scale * scale * dots / D
    g = g_ref[0:M, :].astype(F32) + to_cols(scale) * gn - to_cols(mix) * x_ref[...].astype(F32)
    if len(rest) == 2:
        g = g.astype(BF16).astype(F32) * to_cols(rest[0][0:1, :])
    out_ref[...] = g.astype(BF16)


def dots_kernel(g_ref, p_ref, out_ref):
    g = g_ref[...]
    out_ref[0:M, :] = g
    out_ref[M:R, :] = extra_rows(to_rows(g.astype(F32) * p_ref[...]))


def order_kernel(*refs):
    v, g0, g1, g2 = refs[0:4], refs[4:8], refs[8:12], refs[12:16]
    keep, send = refs[16:20], refs[20:24]
    zh, c = place()
    dp = lax.axis_index("dp")
    zl, y, x = dp // 16, (dp // 4) % 4, dp % 4
    a = jnp.where(c == 0, x, y)

    def at(ia, iz):
        return (zl if iz == 0 else 1 - zl) * 4 + lax.rem(a + 4 - SHIFTS[ia], 4)

    def fill(first, second, q0, q1):
        for ib in range(4):
            for i in range(8):
                q0[ib][i, :, :M] = jnp.transpose(first[ib][i, 0:M, :])
                if second is not None:
                    q1[ib][i, :, :M] = jnp.transpose(second[ib][i, 0:M, :])
            for ia in range(4):
                for iz in range(2):
                    i = at(ia, iz)
                    q0[ib][i, :, M:] = v[ib][ia * 2 + iz, 1]
                    q1[ib][i, :, M:] = v[ib][ia * 2 + iz, 2]
                    if second is None:
                        q1[ib][i, :, :M] = jnp.transpose(v[ib][ia * 2 + iz, 0])

    for half in range(2):
        for core in range(2):
            q0, q1 = (keep, send) if core == 0 else (send, keep)
            first, second = (g0, g1) if half == 0 else (g2, None)
            pl.when(jnp.logical_and(zh == half, c == core))(functools.partial(fill, first, second, q0, q1))


def weight_grad_kernel(*refs):
    keep, recv = refs[0:4], refs[4:8]
    local_ref, far_ref, late_ref, far_late_ref, factor_ref, out_ref, buf, sem = refs[8:]
    zh, c = place()
    late = (zh + c) == 0
    local = jnp.where(late, late_ref[...], local_ref[...])
    far = jnp.where(late, far_late_ref[...], far_ref[...])
    g = jnp.concatenate([local, far], axis=0)
    for features, which, index in ((keep, c, block_index(-1)), (recv, 1 - c, block_index(-1, True))):
        for ib, ref in enumerate(features):
            value = jnp.dot(ref[...].reshape(8 * H, 2 * M), g, preferred_element_type=F32).reshape(8, H, 2 * H)
            for i in range(8):
                j = index(ib, i)
                buf[j, which] = (value[i] * factor_ref[j, which]).astype(BF16)
                pltpu.make_async_copy(buf.at[j, which], out_ref.at[j, which], sem).start()
    pltpu.make_async_copy(buf, out_ref, sem).wait()


def call(kernel, out, specs, args, scratch=(), flops=0, bytes_accessed=0, limit=4, out_specs=None, deps=()):
    count = len(args)

    def body(*refs):
        kernel(*refs[:count], *refs[count + len(deps) :])

    return pl.pallas_call(
        body,
        out_shape=[jax.ShapeDtypeStruct(s, d) for s, d in out],
        in_specs=list(specs) + [pl.BlockSpec(memory_space=pl.ANY)] * len(deps),
        out_specs=out_specs or [VM] * len(out),
        scratch_shapes=list(scratch),
        compiler_params=pltpu.CompilerParams(vmem_limit_bytes=limit * MIB),
        cost_estimate=pl.CostEstimate(flops=flops, bytes_accessed=bytes_accessed, transcendentals=0),
    )(*args, *deps)


MATMUL = dict(
    flops=2 * M * N * H * 2 * H,
    bytes_accessed=4 << 20,
    limit=6,
)


def plane_groups():
    groups = {}
    for i in range(128):
        p, d = divmod(i, 32)
        c = p % 2
        y, x = (d // 4) % 4, d % 4
        groups.setdefault((p, y if c == 0 else x), []).append((d // 16, x if c == 0 else y, i))
    return [[i for _, _, i in sorted(g)] for g in groups.values()]


PLANES = plane_groups()


def core_groups():
    groups = {}
    for i in range(128):
        p, d = divmod(i, 32)
        groups.setdefault((p // 2, (d // 4) % 4), []).append(i)
    return list(groups.values())


CORES = core_groups()


def exchange(value):
    return lax.all_to_all(value, BOTH, 0, 0, axis_index_groups=PLANES)


def along_second(parts):
    return [parts[0]] + [move(parts[i], second_axis(SHIFTS[i])) for i in (1, 2, 3)]


def gather(payload):
    row = exchange(payload)
    return along_second([row] * 4)


def scatter(parts, *deps):
    shape = parts[0].shape
    (total,) = call(sum_kernel, [(shape, BF16)], [VM] * 4, along_second(parts), deps=deps)
    return exchange(total), total


def gather_z(value):
    return jnp.stack([value, move(value, other_zl)])


def gather_first(both, dep):
    rows = [both] + [move(both, first_axis(k)) for k in SHIFTS[1:]]
    return call(join_kernel, [((8,) + both.shape[1:], BF16)], [VM] * 4, rows, deps=(dep,))[0]


def on_device(batches, cotangents, weights, gains, exponents):
    zh, c = place()
    e = zh ^ c
    w5 = weights.reshape(2, N, 2, H, 2 * H)

    def half(value, which):
        return lax.dynamic_slice_in_dim(value, which * H, H, axis=value.ndim - 1)

    own_gain = half(gains[:, 0], c)
    got_gain = move(half(gains[:, 0], 1 - c), other_core)
    gain = []
    for tick in range(4):
        copy_index = zh if tick < 2 else 1 - zh
        own = (e == 0) if tick in (0, 3) else (e == 1)
        both = jnp.where(own, own_gain, got_gain)
        gain.append(lax.dynamic_slice_in_dim(both, copy_index, 1, axis=0))

    x0 = half(lax.dynamic_index_in_dim(batches, zh, axis=0, keepdims=False), c)
    block = (M, H)
    wide = ((8, R, H), BF16)
    out0, ft0 = call(payload_kernel, [wide, (block, BF16)], [VM] * 2, (x0, gain[0]))
    g0 = gather(out0)

    started = move(ft0, other_core)
    own_w, send_w = call(
        split_kernel,
        [((2, N, H, 2 * H), BF16)] * 2,
        [VM],
        (w5,),
        scratch=[pltpu.SemaphoreType.DMA((4,))],
        out_specs=[HBM] * 2,
        limit=10,
        deps=(started,),
    )
    (all_w,) = call(
        pick_kernel,
        [((24, N, H, 2 * H), BF16)],
        [VM] * 2,
        (own_w, move(send_w, other_core)),
        scratch=[pltpu.SemaphoreType.DMA((4,))],
        out_specs=[HBM],
        limit=10,
    )

    def load(tick, *deps):
        return call(
            functools.partial(load_kernel, tick),
            [((N, H, 2 * H), BF16)],
            [HBM],
            (all_w,),
            scratch=[pltpu.SemaphoreType.DMA((8,))],
            deps=deps,
        )[0]

    cot = lax.dynamic_index_in_dim(cotangents, 1 - zh, axis=0, keepdims=False)
    first_parts = call(first_backward_kernel, [((8, H, M), BF16)] * 4, [VM] * 2, (cot, load(3)), **MATMUL)
    parts = along_second(first_parts)

    def forward(weight, gathered, deps):
        keep, send = call(
            forward_kernel, [((M + 8, H), F32)] * 2, [VM] * 5, (*gathered, weight), deps=deps, **MATMUL
        )
        return keep, move(send, other_core)

    outs = [(block, BF16), (block, F32), ((8, M), F32)]
    keep, recv = forward(load(0), g0, ())
    x1, _, s0, out1, ft1 = call(
        combine_kernel, outs + [wide, (block, BF16)], [VM] * 4, (keep, recv, x0, gain[1])
    )
    g1 = gather(out1)
    (row3,) = call(sum_kernel, [((8, H, M), BF16)], [VM] * 4, parts)
    (gn3,) = call(last_sum_kernel, [(block, F32)], [VM] * 2, (exchange(row3), gain[3]))
    keep, recv = forward(load(1, out1), g1, ())
    x2, p1, s1 = call(combine_kernel, outs, [VM] * 4, (keep, recv, x1, gain[1]), deps=(gn3,))
    x2 = move(x2, other_zh)
    out2, ft2 = call(payload_kernel, [wide, (block, BF16)], [VM] * 2, (x2, gain[2]))
    g2 = gather(out2)
    mirror0 = move(jnp.where(zh == 1, ft0, ft2), other_zh)
    keep, recv = forward(load(2, out2), g2, (mirror0,))
    x3, p2, s2, f3, ft3, spread = call(
        third_combine_kernel,
        outs + [(block, BF16), (block, BF16), ((16, 8, M), F32)],
        [VM] * 5,
        (keep, recv, x2, gain[3], gn3),
    )
    (sums,) = call(add_kernel, [((8, M), F32)], [VM], (lax.all_to_all(spread, BOTH, 0, 0, axis_index_groups=CORES),))
    (send3,) = call(choose_kernel, [(block, BF16)], [VM] * 2, (ft3, ft1), deps=(sums,))
    mirror1 = move(send3, other_zh)
    first_rows = gather_z(jnp.stack([f3, mirror0, mirror1]))
    w2 = load(2, x3)
    sums = [sums] + [move(sums, along_y(k)) for k in SHIFTS[1:]]

    mine2, s3, gs3 = call(
        last_grad_kernel,
        [((R, H), BF16), ((8, M), F32), ((M, 2 * H), BF16)],
        [VM] * 8,
        (*sums, cot, gn3, x3, p2),
        deps=(w2, mirror1),
    )

    def backward(weight, mine, s, *deps, extra=()):
        theirs = move(mine, other_core)
        outs = [wide] * 4 + [((M, 2 * H), BF16)] * (2 if extra else 1)
        args = (mine, theirs, s, weight, *extra)
        *parts, last = call(backward_kernel, outs, [VM] * len(args), args, deps=deps, **MATMUL)
        return (parts[:4], *parts[4:], last)

    parts2, gs2 = backward(w2, mine2, s2)
    factor = jnp.repeat(jnp.exp2(-exponents[0].astype(F32)), H, axis=1).reshape(N, 2, 1, 2 * H)
    got2, row2 = scatter(parts2)
    w1 = load(1, row2)
    joined = gather_first(first_rows, row2)
    v = along_second([joined] * 4)
    (back1,) = call(
        grad_kernel,
        [(block, BF16)],
        [VM] * 5,
        (got2, gain[2], mine2, s2, x2),
        deps=(w1,),
    )
    moved1 = move(back1, other_zh)
    (mine1,) = call(dots_kernel, [((R, H), BF16)], [VM] * 2, (moved1, p1), deps=(factor,))
    parts1, local, far = backward(w1, mine1, s1, extra=(gs2, gs3))
    gs1 = local
    keep, send = call(last_forward_kernel, [(block, F32)] * 2, [VM] * 5, (*v, load(3, gs1)), deps=(gs1,), **MATMUL)
    got1, _ = scatter(parts1, keep)
    far = move(far, other_zh)
    turned_features = call(
        order_kernel, [((8, H, 2 * M), BF16)] * 8, [VM] * 16, (*v, *g0, *g1, *g2), limit=14, deps=(gs1,)
    )
    kept, received = turned_features[:4], [move(t, other_core) for t in turned_features[4:]]

    recv = move(send, other_core)
    shown, got = call(last_combine_kernel, [(block, BF16)] * 2, [VM] * 4, (keep, recv, x3, s3))
    got = move(got, other_core)
    last = jnp.where(c == 0, jnp.concatenate([shown, got], 1), jnp.concatenate([got, shown], 1))

    (mine0,) = call(
        grad_kernel,
        [(block, BF16)],
        [VM] * 6,
        (got1, gain[1], mine1, s1, x1, s0),
    )
    late = jnp.concatenate([mine0, move_some(mine0, other_core, [(0, 1), (1, 1)])], axis=1)
    far_late = move_some(late, other_zh, [(1, 0)])
    (total,) = call(
        weight_grad_kernel,
        [((N, 2, H, 2 * H), BF16)],
        [VM] * 13,
        (*kept, *received, local, far, late, far_late, factor),
        scratch=[pltpu.VMEM((N, 2, H, 2 * H), BF16), pltpu.SemaphoreType.DMA],
        out_specs=[HBM],
        flops=2 * 256 * 256 * D,
        bytes_accessed=8 << 20,
        limit=11,
    )
    return (total.reshape(1, D, 2 * H), last[None])


def solution(mesh):
    return jax.shard_map(
        on_device,
        mesh=mesh,
        in_specs=(
            P(None, None, "dp"),
            P(None, None, "dp"),
            P(None, "pipe", None, "dp"),
            P(None, "pipe", "dp"),
            P("pipe", None, "dp"),
        ),
        out_specs=(P("pipe", None, "dp"), P("pipe", None, "dp")),
        check_vma=False,
    )
```
